256 devices in a mesh: tm: 16 (over z_lo, x), rows: 16 (over z_hi, y, core).
Axes of the slice: x: 4, y: 4, z: 8 (z_hi: 2, z_lo: 4; z = z_hi * 4 + z_lo), core: 2. Of those that a mesh axis runs over, the one named last changes fastest.
Arguments:
- initial_warmth: float32 [1024, 1024], P('rows'), may hold values from -6 to 6
- pattern_choice: int32 [32, 8, 8], P('tm'), may hold values from 0 to 7
- dissipation_tables: float32 [8, 128, 128], replicated, may hold values from -6 to 6
- material_label: int32 [8, 8], replicated, may hold values from 0 to 3
- intercept_kappa: float32 [4], replicated, may hold values from 4 to 8
- sensitivity_coef: float32 [4], replicated, may hold values from -0.5 to 0.5
Outputs:
- warmth_trajectory: float32 [32, 1024, 1024], P('tm', 'rows')
The draws below stay inside these ranges and needn't reach their ends.
All inputs are finite; a program needn't handle non-finite values.
Results may differ from the reference program's by a relative error of at most 0.0003.
Values sent between devices are 32-bit elements; how exact they have to be, the bound alone decides.
No kernel may reach another device: no remote copies, remote signals or barrier semaphores. Data moves between devices by JAX's collectives and lax.ppermute only.
A program may use at most 128 MiB of HBM per device.

```python
import math
import jax
import jax.numpy as jnp
from jax import lax

TILES_PER_ROW = 1024
TILES_PER_COLUMN = 1024
TILE = 128
REGIONS = 4
PATTERNS = 8
ITERS = 2
HORIZON_COUNT = 32
TY = 8
TX = 8


def draw_pattern_choice(key, part):
    base_key = jax.random.fold_in(key, 101)
    fresh_key = jax.random.fold_in(key, 202)
    switch_key = jax.random.fold_in(key, 303)
    settled = jax.random.randint(base_key, (TY, TX), 0, PATTERNS)
    fresh = jax.random.randint(fresh_key, (HORIZON_COUNT, TY, TX), 0, PATTERNS)
    switch = jax.random.randint(switch_key, (HORIZON_COUNT, TY, TX), 0, 4)
    return jnp.where(switch == 0, fresh, settled[None]).astype(jnp.int32)


def draw_dissipation_tables(key, part):
    rough_key = jax.random.fold_in(key, 404)
    rough = jax.random.normal(rough_key, (PATTERNS, TILE, TILE), jnp.float32)
    return jnp.clip(rough, -6.0, 6.0).astype(jnp.float32)


def touch_ends(array, key, smallest, top_value):
    spot = [jax.random.randint(jax.random.fold_in(key, axis), (), 0, length) for axis, length in enumerate(array.shape)]
    widest = array.shape.index(max(array.shape))
    neighbour = spot[:widest] + [(spot[widest] + 1) % array.shape[widest]] + spot[widest + 1:]
    return array.at[tuple(spot)].set(smallest).at[tuple(neighbour)].set(top_value)


def level_of(stream_key, extent, cuts, least, largest):
    def one(position, shards_of):
        steps = jax.random.uniform(jax.random.fold_in(jax.random.fold_in(stream_key, 6), position), (shards_of,), jnp.float32, least / len(cuts), largest / len(cuts))
        return jnp.repeat(jnp.exp(steps), extent[position] // shards_of).reshape((-1,) + (1,) * (len(extent) - position - 1))

    factor_of = one(*cuts[0])
    for cut in cuts[1:]:
        factor_of = factor_of * one(*cut)
    return factor_of


def scatter_about(rng, shape, spread, most, cuts=(), kind=jnp.bfloat16):
    drawn = spread * jax.random.normal(rng, shape, jnp.float32)
    if cuts:
        drawn = drawn * level_of(rng, shape, cuts, -0.22, 0.18)
    return jnp.clip(drawn, -most, most).astype(kind)


def setup_inputs(seed: int = 0) -> dict:
    key_of = jax.random.split(jax.random.key(seed), 7)
    return {
        "initial_warmth": scatter_about(key_of[0], (TILES_PER_COLUMN, TILES_PER_ROW), 1.0, 6.0, ((0, 16),), jnp.float32),
        "pattern_choice": draw_pattern_choice(jax.random.fold_in(key_of[6], 71), 0),
        "dissipation_tables": draw_dissipation_tables(jax.random.fold_in(key_of[6], 71), 0),
        "material_label": touch_ends(jax.random.randint(key_of[3], (TY, TX), 0, REGIONS), jax.random.fold_in(key_of[3], 1), 0, REGIONS - 1).astype(jnp.int32),
        "intercept_kappa": jnp.clip(jnp.exp(jax.random.uniform(key_of[4], (REGIONS,), jnp.float32, math.log(4.0), math.log(8.0))), 4.0, 8.0),
        "sensitivity_coef": jnp.clip(jax.random.uniform(key_of[5], (REGIONS,), jnp.float32, -0.5, 0.5), -0.5, 0.5),
    }


TIMESTEP_SIZE = 2.0
ALPHA = 0.05
CROSS_WEIGHT = 1.0 / 64.0


def dct_last(values):
    count = values.shape[-1]
    mirrored = jnp.concatenate([values, jnp.flip(values, -1)], -1)
    spectrum = jnp.fft.fft(mirrored, axis=-1)[..., :count]
    angle = jnp.arange(count).astype(values.dtype) * (math.pi / (2 * count))
    return 0.5 * (jnp.real(spectrum) * jnp.cos(angle) + jnp.imag(spectrum) * jnp.sin(angle))


def idct_last(values):
    count = values.shape[-1]
    angle = jnp.arange(count).astype(values.dtype) * (math.pi / (2 * count))
    weights = jnp.where(jnp.arange(count) == 0, 1.0, 2.0).astype(values.dtype)
    scaled = values * weights
    filled = lax.complex(scaled * jnp.cos(angle), scaled * jnp.sin(angle))
    filled = jnp.concatenate([filled, jnp.zeros_like(filled)], -1)
    return 2.0 * jnp.real(jnp.fft.ifft(filled, axis=-1))[..., :count]


def both_forward(values):
    inner = dct_last(values)
    return jnp.swapaxes(dct_last(jnp.swapaxes(inner, 1, 2)), 1, 2)


def both_inverse(values):
    inner = jnp.swapaxes(idct_last(jnp.swapaxes(values, 1, 2)), 1, 2)
    return idct_last(inner)


def reference(initial_warmth, pattern_choice, dissipation_tables, material_label, intercept_kappa, sensitivity_coef):
    tiles = dissipation_tables[pattern_choice]
    forcing_term = jnp.transpose(tiles, (0, 1, 3, 2, 4)).reshape(HORIZON_COUNT, TILES_PER_COLUMN, TILES_PER_ROW)
    reference_level = jnp.repeat(jnp.repeat(intercept_kappa[material_label], TILE, 0), TILE, 1)
    kappa_derivative = jnp.repeat(jnp.repeat(sensitivity_coef[material_label], TILE, 0), TILE, 1)
    conduct = jnp.mean(intercept_kappa)
    amplification = jnp.exp(jnp.arange(HORIZON_COUNT).astype(jnp.float32) * (math.log(ALPHA) / HORIZON_COUNT))
    shrink = ALPHA ** (1.0 / HORIZON_COUNT)
    theta = jnp.arange(HORIZON_COUNT).astype(jnp.float32) * (2.0 * math.pi / HORIZON_COUNT)
    mu_rows = 2.0 - 2.0 * jnp.cos(jnp.arange(TILES_PER_COLUMN).astype(jnp.float32) * (math.pi / TILES_PER_COLUMN))
    mu_cols = 2.0 - 2.0 * jnp.cos(jnp.arange(TILES_PER_ROW).astype(jnp.float32) * (math.pi / TILES_PER_ROW))
    real_den = (1.0 - shrink * jnp.cos(theta))[:, None, None] / TIMESTEP_SIZE + conduct * (mu_rows[None, :, None] + CROSS_WEIGHT * mu_cols[None, None, :])
    imag_den = (shrink * jnp.sin(theta) / TIMESTEP_SIZE)[:, None, None]
    norm_den = real_den * real_den + imag_den * imag_den
    warmth_trajectory = jnp.broadcast_to(initial_warmth[None], (HORIZON_COUNT, TILES_PER_COLUMN, TILES_PER_ROW)).astype(jnp.float32)
    for sweep in range(ITERS):
        kappa_local = reference_level * (1.0 + kappa_derivative * jnp.tanh(warmth_trajectory))
        upward_current = 0.5 * (kappa_local[:, 1:] + kappa_local[:, :-1]) * (warmth_trajectory[:, 1:] - warmth_trajectory[:, :-1])
        lateral_current = CROSS_WEIGHT * (0.5 * (kappa_local[:, :, 1:] + kappa_local[:, :, :-1]) * (warmth_trajectory[:, :, 1:] - warmth_trajectory[:, :, :-1]))
        energy_ledger = jnp.pad(upward_current, ((0, 0), (0, 1), (0, 0))) - jnp.pad(upward_current, ((0, 0), (1, 0), (0, 0)))
        energy_ledger = energy_ledger + jnp.pad(lateral_current, ((0, 0), (0, 0), (0, 1))) - jnp.pad(lateral_current, ((0, 0), (0, 0), (1, 0)))
        former_warmth = jnp.concatenate([initial_warmth[None], warmth_trajectory[:-1]], 0)
        defect_vector = forcing_term - (warmth_trajectory - former_warmth) / TIMESTEP_SIZE + energy_ledger
        scaled = defect_vector * amplification[:, None, None]
        spectrum = jnp.fft.fft(scaled, axis=0)
        modes_re = both_forward(jnp.real(spectrum))
        modes_im = both_forward(jnp.imag(spectrum))
        solved_re = (modes_re * real_den + modes_im * imag_den) / norm_den
        solved_im = (modes_im * real_den - modes_re * imag_den) / norm_den
        field_re = both_inverse(solved_re)
        field_im = both_inverse(solved_im)
        correction_delta = jnp.real(jnp.fft.ifft(lax.complex(field_re, field_im), axis=0))
        warmth_trajectory = warmth_trajectory + correction_delta / amplification[:, None, None]
    return warmth_trajectory
```

```python
import functools
import math

import jax
import jax.numpy as jnp
import ml_dtypes
import numpy as np
from jax import lax
from jax.experimental import pallas as pl
from jax.experimental.pallas import tpu as pltpu
from jax.sharding import PartitionSpec as P

TILE = 128
SIZE = 1024
STEPS = 32
STRIP = 64
DEVICES = 256
ALPHA = 0.05
CROSS_WEIGHT = 1.0 / 64.0
P_BLOCK = 256
BOTH = ("tm", "rows")
F32 = jnp.float32
BF16 = jnp.bfloat16
VMEM_LIMIT = 56 * 1024 * 1024


def halves(table):
    high = table.astype(ml_dtypes.bfloat16)
    low = (table - high.astype(np.float64)).astype(ml_dtypes.bfloat16)
    return high, low


@functools.cache
def constants():
    k = np.arange(SIZE, dtype=np.int64)
    phase = k[:, None] * (2 * k[None, :] + 1) % (4 * SIZE)
    cosines = np.cos(phase.astype(np.float64) * (math.pi / (2 * SIZE)))
    made = {}
    made["g"] = halves(cosines)
    made["gt"] = halves(np.ascontiguousarray(cosines.T))
    made["by_mode"] = halves(np.ascontiguousarray(cosines.reshape(DEVICES, 4, SIZE).swapaxes(0, 1)))
    made["own"] = halves(cosines.reshape(DEVICES, 32, TILE))
    mu = 2.0 - 2.0 * np.cos(np.arange(SIZE) * (math.pi / SIZE))
    made["mu_p"] = mu[None, :].astype(np.float32)
    own_mu = np.tile(mu.reshape(DEVICES, 4), (1, 2))
    made["mu_q"] = np.repeat(own_mu[:, :, None], 128, 2).astype(np.float32)
    weights = np.full((1, SIZE), 2.0 / SIZE, np.float32)
    weights[0, 0] = 1.0 / SIZE
    made["w_p"] = weights
    own_w = np.tile(weights.reshape(DEVICES, 4), (1, 2))
    made["w_q"] = np.repeat(own_w[:, :, None], 128, 2).astype(np.float32)
    pick = np.zeros((8, 144, 256), np.float32)
    spread = np.zeros((8, 144, 128), np.float32)
    for ty in range(8):
        for row in range(128):
            pick[ty, row, (row // 4) * 8 + ty] = 1.0
        for row in range(128, 144):
            for half in range(2):
                spread[ty, row, half * 64 + (row % 4) * 16 + 2 * ty + half] = 1.0
    made["pick"] = pick.reshape(1152, 256).astype(ml_dtypes.bfloat16)
    made["spread"] = spread.reshape(1152, 128).astype(ml_dtypes.bfloat16)
    return made


def split(values):
    high = values.astype(BF16)
    return high, (values - high.astype(F32)).astype(BF16)


def dot(a, b):
    return jnp.dot(a, b, preferred_element_type=F32)


def dot_nt(a, b):
    return lax.dot_general(a, b, (((1,), (1,)), ((), ())), preferred_element_type=F32)


def dot3(a, b, product=dot):
    return product(a[0], b[0]) + product(a[0], b[1]) + product(a[1], b[0])


def iota(shape, dim):
    return lax.broadcasted_iota(jnp.int32, shape, dim)


def block_swap(tiles):
    shape = tiles.shape
    swapped = pltpu.roll(pltpu.roll(tiles, 4, axis=1), 64, axis=2)
    diagonal = (iota(shape, 1) < 4) == (iota(shape, 2) < 64)
    return jnp.where(diagonal, tiles, swapped)


def material_row(labels, values, ty):
    return jnp.concatenate(
        [jnp.full((1, TILE), values[labels[ty, tx]], F32) for tx in range(8)], 1
    )


def divergence(w, above, below, r, labels, intercept, sensitivity):
    first = r * STRIP
    ty = first // TILE
    ty_above = jnp.maximum(first - 1, 0) // TILE
    ty_below = jnp.minimum(first + STRIP, SIZE - 1) // TILE

    def kappa(values, where_ty):
        base = material_row(labels, intercept, where_ty)
        slope = material_row(labels, sensitivity, where_ty)
        return base * (1.0 + slope * jnp.tanh(values))

    k = kappa(w, ty)
    k_above = kappa(above, ty_above)
    k_below = kappa(below, ty_below)
    shape = w.shape
    row, column = iota(shape, 0), iota(shape, 1)
    last = row == STRIP - 1
    w_next = jnp.where(last, below, pltpu.roll(w, STRIP - 1, axis=0))
    k_next = jnp.where(last, k_below, pltpu.roll(k, STRIP - 1, axis=0))
    down = 0.5 * (k + k_next) * (w_next - w)
    down = jnp.where(last & (r == SIZE // STRIP - 1), 0.0, down)
    entry = 0.5 * (k_above + k[:1]) * (w[:1] - above)
    entry = jnp.where(r == 0, 0.0, entry)
    up = jnp.where(row == 0, entry, pltpu.roll(down, 1, axis=0))
    w_right = pltpu.roll(w, SIZE - 1, axis=1)
    k_right = pltpu.roll(k, SIZE - 1, axis=1)
    side = CROSS_WEIGHT * (0.5 * (k + k_right) * (w_right - w))
    side = jnp.where(column == SIZE - 1, 0.0, side)
    return down - up + (side - pltpu.roll(side, 1, axis=1))


def start_kernel(
    pos, labels, intercept, sensitivity, patterns, w_ref, above, below, table_hi, table_lo, out
):
    r = pos[1]
    d = divergence(w_ref[...], above[...], below[...], r, labels, intercept, sensitivity)
    padded = jnp.concatenate([jnp.zeros_like(d), d], 0)
    modes = dot3((table_hi[...], table_lo[...]), split(padded), dot_nt)
    lane = iota((1, 128), 1)
    chosen = jnp.zeros((1, 128), jnp.int32)
    for tx in range(8):
        chosen = jnp.where(lane % 8 == tx, patterns[r, tx], chosen)
    one_hot = jnp.where((chosen == lane // 8) & (lane < 64), 1.0, 0.0).astype(F32)
    out[...] = modes + one_hot


def cyclic_solve(force, rho, store):
    even = iota(rho.shape, 0) < 4
    z = jnp.zeros_like(rho)
    twice = 2.0 * rho
    for tile in range(STEPS // 2):
        drive = twice * force(tile)
        v = rho * pltpu.roll(z, 4, axis=0) + drive
        z = rho * pltpu.roll(v, 4, axis=0) + drive
    power = rho
    for _ in range(5):
        power = power * power
    u = ALPHA * z / (1.0 - ALPHA * power)
    for tile in range(STEPS // 2):
        drive = twice * force(tile)
        v = rho * pltpu.roll(u, 4, axis=0) + drive
        other = rho * pltpu.roll(v, 4, axis=0) + drive
        u = jnp.where(even, v, other)
        store(tile, u)


def damping(intercept, mu_p, mu_q):
    count = intercept.shape[0]
    conduct = intercept[0]
    for region in range(1, count):
        conduct = conduct + intercept[region]
    conduct = conduct / count
    kappa = conduct * (mu_p[...] + CROSS_WEIGHT * mu_q[...][:, :1])
    return 1.0 / (1.0 + 2.0 * kappa)


def give_back(step, u_ref, w_p, w_q, table_hi, table_lo, total, out):
    scale = w_p[...] * w_q[...][:, :1]
    u = u_ref[...].reshape(STEPS // 2, 8, P_BLOCK) * scale[None]
    part = dot3(split(u.reshape(128, P_BLOCK)), (table_hi[...], table_lo[...]))

    @pl.when(step == 0)
    def _():
        total[...] = part

    @pl.when(step != 0)
    def _():
        total[...] += part

    @pl.when(step == SIZE // P_BLOCK - 1)
    def _():
        for j in range(8):
            tiles = total[:, j * 128 : (j + 1) * 128].reshape(16, 8, 128)
            out[:, j] = block_swap(tiles)


def first_solve_kernel(
    pos,
    intercept,
    received,
    tables,
    own_hi,
    own_lo,
    pick,
    spread,
    mu_p,
    mu_q,
    w_p,
    w_q,
    gt_hi,
    gt_lo,
    g_hi,
    g_lo,
    out,
    update,
    rest,
    x_hi,
    x_lo,
    total,
):
    step = pl.program_id(0)

    @pl.when(step == 0)
    def _():
        got = received[...]
        lane = iota((256, 128), 1)
        rolled = pltpu.roll(got, 64, axis=1)
        doubled = jnp.where(lane < 64, got, rolled).astype(BF16)
        chosen = dot(pick[...], jnp.concatenate([doubled, doubled], 1))
        match = (iota((1152, 256), 0) % 4) == (iota((1152, 256), 1) // 64)
        chosen = jnp.where(match, chosen, 0.0).astype(BF16)
        by_tile = dot3((own_hi[...], own_lo[...]), split(tables[...]), dot_nt)
        pieces = [
            by_tile[q * 8 : (q + 1) * 8, k * 128 : (k + 1) * 128]
            for q in range(4)
            for k in range(8)
        ]
        a_hi, a_lo = split(jnp.concatenate(pieces, 0))
        low_lane = lane[:64] < 64
        top = jnp.where(low_lane, rolled[:64], 0.0)
        bottom = jnp.where(low_lane, 0.0, got[:64])
        d_hi, d_lo = split(jnp.concatenate([top, bottom], 0))
        spread_rows = spread[...]
        both = dot(chosen, a_hi) + dot(chosen, a_lo)
        both = both + (dot(spread_rows, d_hi) + dot(spread_rows, d_lo))
        for ty in range(8):
            hi, lo = split(both[ty * 144 : (ty + 1) * 144])
            x_hi[:, ty * 128 : (ty + 1) * 128] = hi
            x_lo[:, ty * 128 : (ty + 1) * 128] = lo

    modes = dot3((x_hi[...], x_lo[...]), (gt_hi[...], gt_lo[...]))
    shared = modes[128:136]
    rho = damping(intercept, mu_p, mu_q)
    even = iota(rho.shape, 0) < 4
    last = [jnp.zeros_like(rho)]

    def force(tile):
        return modes[tile * 8 : tile * 8 + 8] + shared

    def store(tile, u):
        rows = slice(tile * 8, tile * 8 + 8)
        update[rows, :] = u
        turned = pltpu.roll(u, 4, axis=0)
        earlier = jnp.where(even, last[0], turned)
        rest[rows, :] = modes[rows] - 0.5 * (u - earlier)
        last[0] = turned

    cyclic_solve(force, rho, store)
    give_back(step, update, w_p, w_q, g_hi, g_lo, total, out)


def second_solve_kernel(
    pos,
    intercept,
    received,
    before,
    rest,
    mu_p,
    mu_q,
    w_p,
    w_q,
    gt_hi,
    gt_lo,
    g_hi,
    g_lo,
    out,
    x_hi,
    x_lo,
    update,
    total,
):
    step = pl.program_id(0)

    @pl.when(step == 0)
    def _():
        for j in range(8):
            tiles = block_swap(received[:, j])
            hi, lo = split(tiles.reshape(128, 128))
            x_hi[:, j * 128 : (j + 1) * 128] = hi
            x_lo[:, j * 128 : (j + 1) * 128] = lo

    modes = dot3((x_hi[...], x_lo[...]), (gt_hi[...], gt_lo[...])) + rest[...]
    rho = damping(intercept, mu_p, mu_q)

    def force(tile):
        return modes[tile * 8 : tile * 8 + 8]

    def store(tile, u):
        rows = slice(tile * 8, tile * 8 + 8)
        update[rows, :] = u + before[rows, :]

    cyclic_solve(force, rho, store)
    give_back(step, update, w_p, w_q, g_hi, g_lo, total, out)


def warmth_kernel(received, g_hi, g_lo, initial, out):
    rows = split(received[...].T)
    update = dot3(rows, (g_hi[...], g_lo[...]))
    start = initial[...]
    out[0] = update[:STRIP] + start
    out[1] = update[STRIP:] + start


def divergence_kernel(
    pos, labels, intercept, sensitivity, warmth, above, below, g_hi, g_lo, out, d_ref
):
    for n in range(2):
        d_ref[n * STRIP : (n + 1) * STRIP, :] = divergence(
            warmth[n],
            above[n : n + 1],
            below[n : n + 1],
            pos[1],
            labels,
            intercept,
            sensitivity,
        )
    out[...] = dot3((g_hi[...], g_lo[...]), split(d_ref[...]), dot_nt)


def whole(shape):
    return pl.BlockSpec(shape, lambda i, *_: (0,) * len(shape))


SMEM = pl.BlockSpec(memory_space=pltpu.SMEM)


def call(kernel, pos, grid, in_specs, out_specs, out_shape, scratch, *args):
    spec = pltpu.PrefetchScalarGridSpec(
        num_scalar_prefetch=1,
        grid=(grid,),
        in_specs=in_specs,
        out_specs=out_specs,
        scratch_shapes=scratch,
    )
    return pl.pallas_call(
        kernel,
        grid_spec=spec,
        out_shape=out_shape,
        compiler_params=pltpu.CompilerParams(vmem_limit_bytes=VMEM_LIMIT),
    )(pos, *args)


def own_block(rows):
    return pl.BlockSpec((None, rows, 128), lambda i, pos: (pos[2], 0, 0))


def exchange(tiles):
    return lax.all_to_all(tiles, BOTH, split_axis=0, concat_axis=0, tiled=True)


def shape_of(*dims):
    return jax.ShapeDtypeStruct(dims, F32)


def shards(
    initial_warmth,
    pattern_choice,
    dissipation_tables,
    material_label,
    intercept_kappa,
    sensitivity_coef,
):
    made = constants()
    t, r = lax.axis_index("tm"), lax.axis_index("rows")
    rows_count = lax.axis_size("rows")
    pos = jnp.stack([t, r, t * rows_count + r]).astype(jnp.int32)
    forward = [(i, i + 1) for i in range(rows_count - 1)]
    backward = [(i + 1, i) for i in range(rows_count - 1)]

    def neighbours(first, last):
        return (
            lax.ppermute(last, "rows", forward),
            lax.ppermute(first, "rows", backward),
        )

    g, gt = made["g"], made["gt"]
    material = (material_label, intercept_kappa, sensitivity_coef)
    above, below = neighbours(initial_warmth[:1], initial_warmth[-1:])
    by_mode = pl.BlockSpec((None, 256, SIZE), lambda i, pos: (lax.rem(pos[0], 4), 0, 0))
    started = call(
        start_kernel,
        pos,
        1,
        [SMEM] * 4 + [whole((STRIP, SIZE)), whole((1, SIZE)), whole((1, SIZE)), by_mode, by_mode],
        whole((256, 128)),
        shape_of(256, 128),
        [],
        *material,
        pattern_choice.reshape(16, 8),
        initial_warmth,
        above,
        below,
        *made["by_mode"],
    )
    received = exchange(started.reshape(256, 1, 128)).reshape(256, 128)

    p_row = pl.BlockSpec((1, P_BLOCK), lambda i, pos: (0, i))
    p_block = pl.BlockSpec((128, P_BLOCK), lambda i, pos: (0, i))
    gt_block = pl.BlockSpec((SIZE, P_BLOCK), lambda i, pos: (0, i))
    g_block = pl.BlockSpec((P_BLOCK, SIZE), lambda i, pos: (i, 0))
    spectral = [p_row, own_block(8), p_row, own_block(8), gt_block, gt_block, g_block, g_block]
    spectral_args = (made["mu_p"], made["mu_q"], made["w_p"], made["w_q"], *gt, *g)
    steps = SIZE // P_BLOCK
    sent, before, rest = call(
        first_solve_kernel,
        pos,
        steps,
        [
            SMEM,
            whole((256, 128)),
            whole((SIZE, 128)),
            own_block(32),
            own_block(32),
            whole((1152, 256)),
            whole((1152, 128)),
            *spectral,
        ],
        [whole((16, 8, 8, 128)), p_block, p_block],
        [shape_of(16, 8, 8, 128), shape_of(128, SIZE), shape_of(128, SIZE)],
        [
            pltpu.VMEM((144, SIZE), BF16),
            pltpu.VMEM((144, SIZE), BF16),
            pltpu.VMEM((128, SIZE), F32),
        ],
        intercept_kappa,
        received,
        dissipation_tables.reshape(SIZE, 128),
        *made["own"],
        made["pick"],
        made["spread"],
        *spectral_args,
    )
    received = exchange(sent.reshape(256, 4, 128)).reshape(SIZE, 128)
    table = whole((SIZE, SIZE))

    def warmth_of(received):
        return pl.pallas_call(
            warmth_kernel,
            grid=(1,),
            in_specs=[whole((SIZE, 128)), table, table, whole((STRIP, SIZE))],
            out_specs=whole((2, STRIP, SIZE)),
            out_shape=shape_of(2, STRIP, SIZE),
            compiler_params=pltpu.CompilerParams(vmem_limit_bytes=VMEM_LIMIT),
        )(received, *g, initial_warmth)

    warmth = warmth_of(received)
    above, below = neighbours(warmth[:, 0], warmth[:, -1])
    sent = call(
        divergence_kernel,
        pos,
        1,
        [SMEM] * 3 + [whole((2, STRIP, SIZE)), whole((2, SIZE)), whole((2, SIZE)), table, table],
        whole((SIZE, 128)),
        shape_of(SIZE, 128),
        [pltpu.VMEM((128, SIZE), F32)],
        *material,
        warmth,
        above,
        below,
        *g,
    )
    received = exchange(sent.reshape(256, 4, 128)).reshape(16, 8, 8, 128)
    sent = call(
        second_solve_kernel,
        pos,
        steps,
        [SMEM, whole((16, 8, 8, 128)), p_block, p_block, *spectral],
        whole((16, 8, 8, 128)),
        shape_of(16, 8, 8, 128),
        [
            pltpu.VMEM((128, SIZE), BF16),
            pltpu.VMEM((128, SIZE), BF16),
            pltpu.VMEM((128, P_BLOCK), F32),
            pltpu.VMEM((128, SIZE), F32),
        ],
        intercept_kappa,
        received,
        before,
        rest,
        *spectral_args,
    )
    received = exchange(sent.reshape(256, 4, 128)).reshape(SIZE, 128)
    return warmth_of(received)


def solution(mesh):
    in_specs = (P("rows", None), P("tm", None, None), P(), P(), P(), P())
    out_specs = P("tm", "rows", None)
    return jax.shard_map(shards, mesh=mesh, in_specs=in_specs, out_specs=out_specs, check_vma=False)
```

```python
import functools
import math

import jax
import jax.numpy as jnp
import ml_dtypes
import numpy as np
from jax import lax
from jax.experimental import pallas as pl
from jax.experimental.pallas import tpu as pltpu
from jax.sharding import PartitionSpec as P

TILE = 128
SIZE = 1024
STEPS = 32
STRIP = 64
DEVICES = 256
ALPHA = 0.05
CROSS_WEIGHT = 1.0 / 64.0
P_BLOCK = 256
BOTH = ("tm", "rows")
F32 = jnp.float32
BF16 = jnp.bfloat16
VMEM_LIMIT = 56 * 1024 * 1024


def halves(table):
    high = table.astype(ml_dtypes.bfloat16)
    low = (table - high.astype(np.float64)).astype(ml_dtypes.bfloat16)
    return high, low


@functools.cache
def constants():
    k = np.arange(SIZE, dtype=np.int64)
    phase = k[:, None] * (2 * k[None, :] + 1) % (4 * SIZE)
    cosines = np.cos(phase.astype(np.float64) * (math.pi / (2 * SIZE)))
    made = {}
    made["g"] = halves(cosines)
    made["gt"] = halves(np.ascontiguousarray(cosines.T))
    made["by_mode"] = halves(np.ascontiguousarray(cosines.reshape(DEVICES, 4, SIZE).swapaxes(0, 1)))
    edge_rows = np.concatenate([np.arange(-1, SIZE - 1, STRIP), np.arange(STRIP, SIZE + 1, STRIP)])
    inside = (edge_rows >= 0) & (edge_rows < SIZE)
    made["edge"] = halves(cosines.T[np.clip(edge_rows, 0, SIZE - 1)] * inside[:, None])
    made["own"] = halves(cosines.reshape(DEVICES, 32, TILE))
    mu = 2.0 - 2.0 * np.cos(np.arange(SIZE) * (math.pi / SIZE))
    made["mu_p"] = mu[None, :].astype(np.float32)
    own_mu = np.tile(mu.reshape(DEVICES, 4), (1, 2))
    made["mu_q"] = np.repeat(own_mu[:, :, None], 128, 2).astype(np.float32)
    weights = np.full((1, SIZE), 2.0 / SIZE, np.float32)
    weights[0, 0] = 1.0 / SIZE
    made["w_p"] = weights
    own_w = np.tile(weights.reshape(DEVICES, 4), (1, 2))
    made["w_q"] = np.repeat(own_w[:, :, None], 128, 2).astype(np.float32)
    pick = np.zeros((8, 144, 256), np.float32)
    spread = np.zeros((8, 144, 128), np.float32)
    for ty in range(8):
        for row in range(128):
            pick[ty, row, (row // 4) * 8 + ty] = 1.0
        for row in range(128, 144):
            for half in range(2):
                spread[ty, row, half * 64 + (row % 4) * 16 + 2 * ty + half] = 1.0
    made["pick"] = pick.reshape(1152, 256).astype(ml_dtypes.bfloat16)
    made["spread"] = spread.reshape(1152, 128).astype(ml_dtypes.bfloat16)
    return made


def split(values):
    high = values.astype(BF16)
    return high, (values - high.astype(F32)).astype(BF16)


def dot(a, b):
    return jnp.dot(a, b, preferred_element_type=F32)


def dot_nt(a, b):
    return lax.dot_general(a, b, (((1,), (1,)), ((), ())), preferred_element_type=F32)


def dot3(a, b, product=dot):
    return product(a[0], b[0]) + product(a[0], b[1]) + product(a[1], b[0])


def iota(shape, dim):
    return lax.broadcasted_iota(jnp.int32, shape, dim)


def block_swap(tiles):
    shape = tiles.shape
    swapped = pltpu.roll(pltpu.roll(tiles, 4, axis=1), 64, axis=2)
    diagonal = (iota(shape, 1) < 4) == (iota(shape, 2) < 64)
    return jnp.where(diagonal, tiles, swapped)


def material_row(labels, values, ty):
    return jnp.concatenate(
        [jnp.full((1, TILE), values[labels[ty, tx]], F32) for tx in range(8)], 1
    )


def conductivity(values, base, slope):
    return base * (1.0 + slope * jnp.tanh(values))


def inner_divergence(w, k, above=None, below=None):
    shape = w.shape
    row, column = iota(shape, 0), iota(shape, 1)
    w_next = pltpu.roll(w, STRIP - 1, axis=0)
    k_next = pltpu.roll(k, STRIP - 1, axis=0)
    below = jnp.zeros((1, 1), F32) if below is None else below
    above = jnp.zeros((1, 1), F32) if above is None else above
    down = jnp.where(row == STRIP - 1, below, 0.5 * (k + k_next) * (w_next - w))
    up = jnp.where(row == 0, above, pltpu.roll(down, 1, axis=0))
    w_right = pltpu.roll(w, SIZE - 1, axis=1)
    k_right = pltpu.roll(k, SIZE - 1, axis=1)
    side = CROSS_WEIGHT * (0.5 * (k + k_right) * (w_right - w))
    side = jnp.where(column == SIZE - 1, 0.0, side)
    return down - up + (side - pltpu.roll(side, 1, axis=1))


def material_rows(labels, values, ty):
    return material_row(labels, values[0], ty), material_row(labels, values[1], ty)


def start_kernel(
    pos, labels, intercept, sensitivity, patterns, w_ref, table_hi, table_lo, out
):
    t, r = pos[0], pos[1]
    w = w_ref[...]
    base, slope = material_rows(labels, (intercept, sensitivity), r * STRIP // TILE)
    d = inner_divergence(w, conductivity(w, base, slope))
    padded = jnp.concatenate([jnp.zeros_like(d), d], 0)
    modes = dot3((table_hi[...], table_lo[...]), split(padded), dot_nt)
    lane = iota((1, 128), 1)
    chosen = jnp.zeros((1, 128), jnp.int32)
    for tx in range(8):
        chosen = jnp.where(lane % 8 == tx, patterns[r, tx], chosen)
    one_hot = jnp.where((chosen == lane // 8) & (lane < 64), 1.0, 0.0).astype(F32)
    out[pl.ds(0, 256, stride=2), :] = modes + one_hot
    columns = pl.ds(pl.multiple_of(t // 2 * 128, 128), 128)
    first, last = w_ref[0:1, columns], w_ref[STRIP - 1 : STRIP, columns]
    first = jnp.where(t % 2 == 0, first, pltpu.roll(first, 64, axis=1))
    last = jnp.where(t % 2 == 0, pltpu.roll(last, 64, axis=1), last)
    edges = jnp.where(lane < 64, first, last)
    out[pl.ds(1, 256, stride=2), :] = jnp.broadcast_to(edges, (256, 128))


def face_fluxes(got, labels, intercept, sensitivity, own, first_ref, last_ref):
    lane = iota((16, 128), 1) < 64
    row = iota((16, 128), 0)
    totals = [jnp.zeros((16, 128), F32)] * 4
    for tx in range(8):
        columns = slice(tx * 128, tx * 128 + 128)
        left = got[tx * 32 : tx * 32 + 16]
        right = got[tx * 32 + 16 : tx * 32 + 32]
        first = jnp.where(lane, left, pltpu.roll(right, 64, axis=1))
        last = jnp.where(lane, pltpu.roll(left, 64, axis=1), right)
        first_ref[:, columns] = first
        last_ref[:, columns] = last
        base = jnp.zeros((16, 128), F32)
        slope = jnp.zeros((16, 128), F32)
        for ty in range(8):
            here = row // 2 == ty
            base = jnp.where(here, intercept[labels[ty, tx]], base)
            slope = jnp.where(here, sensitivity[labels[ty, tx]], slope)
        k_first = conductivity(first, base, slope)
        k_last = conductivity(last, base, slope)
        w_next = pltpu.roll(first, 15, axis=0)
        k_next = pltpu.roll(k_first, 15, axis=0)
        flux = jnp.where(row == 15, 0.0, 0.5 * (k_last + k_next) * (w_next - last))
        for q in range(4):
            totals[q] = totals[q] + own[q * 8 + tx : q * 8 + tx + 1, :] * flux
    sums = [jnp.sum(total, axis=1, keepdims=True) for total in totals]
    down = jnp.concatenate(sums, 0)
    up = jnp.concatenate([pltpu.roll(jnp.broadcast_to(x, (16, 128)), 1, axis=0) for x in sums], 0)
    return down, up[:, :1]


def cyclic_solve(force, rho, store):
    even = iota(rho.shape, 0) < 4
    z = jnp.zeros_like(rho)
    twice = 2.0 * rho
    for tile in range(STEPS // 2):
        drive = twice * force(tile)
        v = rho * pltpu.roll(z, 4, axis=0) + drive
        z = rho * pltpu.roll(v, 4, axis=0) + drive
    power = rho
    for _ in range(5):
        power = power * power
    u = ALPHA * z / (1.0 - ALPHA * power)
    for tile in range(STEPS // 2):
        drive = twice * force(tile)
        v = rho * pltpu.roll(u, 4, axis=0) + drive
        other = rho * pltpu.roll(v, 4, axis=0) + drive
        u = jnp.where(even, v, other)
        store(tile, u)


def damping(intercept, mu_p, mu_q):
    count = intercept.shape[0]
    conduct = intercept[0]
    for region in range(1, count):
        conduct = conduct + intercept[region]
    conduct = conduct / count
    kappa = conduct * (mu_p[...] + CROSS_WEIGHT * mu_q[...][:, :1])
    return 1.0 / (1.0 + 2.0 * kappa)


def accumulate(step, total, part):
    @pl.when(step == 0)
    def _():
        total[...] = part

    @pl.when(step != 0)
    def _():
        total[...] += part


def weighted(u_ref, w_p, w_q):
    scale = w_p[...] * w_q[...][:, :1]
    u = u_ref[...].reshape(STEPS // 2, 8, P_BLOCK) * scale[None]
    return split(u.reshape(128, P_BLOCK))


def first_solve_kernel(
    pos,
    labels,
    intercept,
    sensitivity,
    received,
    tables,
    own_hi,
    own_lo,
    edge_hi,
    edge_lo,
    pick,
    spread,
    mu_p,
    mu_q,
    w_p,
    w_q,
    gt_hi,
    gt_lo,
    g_hi,
    g_lo,
    out,
    update,
    rest,
    near,
    x_hi,
    x_lo,
    total,
    edge_total,
    rows,
    first_ref,
    last_ref,
):
    step = pl.program_id(0)

    @pl.when(step == 0)
    def _():
        got = received[pl.ds(0, 256, stride=2), :]
        edges = received[pl.ds(1, 256, stride=2), :]
        own = own_hi[...].astype(F32) + own_lo[...].astype(F32)
        down, up = face_fluxes(edges, labels, intercept, sensitivity, own, first_ref, last_ref)
        strip = iota((16, SIZE), 0)
        r = pos[1]
        near[0:1, :] = jnp.sum(jnp.where(strip == r - 1, last_ref[...], 0.0), 0, keepdims=True)
        near[1:2, :] = jnp.sum(jnp.where(strip == r + 1, first_ref[...], 0.0), 0, keepdims=True)
        near[2:8, :] = jnp.zeros((6, SIZE), F32)
        lane = iota((256, 128), 1)
        rolled = pltpu.roll(got, 64, axis=1)
        doubled = jnp.where(lane < 64, got, rolled).astype(BF16)
        chosen = dot(pick[...], jnp.concatenate([doubled, doubled], 1))
        match = (iota((1152, 256), 0) % 4) == (iota((1152, 256), 1) // 64)
        chosen = jnp.where(match, chosen, 0.0).astype(BF16)
        by_tile = dot3((own_hi[...], own_lo[...]), split(tables[...]), dot_nt)
        pieces = [
            by_tile[q * 8 : (q + 1) * 8, k * 128 : (k + 1) * 128]
            for q in range(4)
            for k in range(8)
        ]
        a_hi, a_lo = split(jnp.concatenate(pieces, 0))
        few = lane[:64]
        inner = got[:64]
        inner = inner + jnp.where(few == 127, down, 0.0) - jnp.where(few == 64, up, 0.0)
        top = jnp.where(few < 64, pltpu.roll(inner, 64, axis=1), 0.0)
        bottom = jnp.where(few < 64, 0.0, inner)
        d_hi, d_lo = split(jnp.concatenate([top, bottom], 0))
        spread_rows = spread[...]
        both = dot(chosen, a_hi) + dot(chosen, a_lo)
        both = both + (dot(spread_rows, d_hi) + dot(spread_rows, d_lo))
        for ty in range(8):
            hi, lo = split(both[ty * 144 : (ty + 1) * 144])
            x_hi[:, ty * 128 : (ty + 1) * 128] = hi
            x_lo[:, ty * 128 : (ty + 1) * 128] = lo

    modes = dot3((x_hi[...], x_lo[...]), (gt_hi[...], gt_lo[...]))
    shared = modes[128:136]
    rho = damping(intercept, mu_p, mu_q)
    even = iota(rho.shape, 0) < 4
    last = [jnp.zeros_like(rho)]

    def force(tile):
        return modes[tile * 8 : tile * 8 + 8] + shared

    def store(tile, u):
        rows = slice(tile * 8, tile * 8 + 8)
        update[rows, :] = u
        turned = pltpu.roll(u, 4, axis=0)
        earlier = jnp.where(even, last[0], turned)
        rest[rows, :] = modes[rows] - 0.5 * (u - earlier)
        last[0] = turned

    cyclic_solve(force, rho, store)
    u = weighted(update, w_p, w_q)
    accumulate(step, total, dot3(u, (g_hi[...], g_lo[...])))
    accumulate(step, edge_total, dot3((edge_hi[...], edge_lo[...]), u, dot_nt))

    @pl.when(step == SIZE // P_BLOCK - 1)
    def _():
        for j in range(8):
            tiles = total[:, j * 128 : (j + 1) * 128].reshape(16, 8, 128)
            rows[:, j] = block_swap(tiles)
        flat = rows.reshape(SIZE, 128)
        for q in range(4):
            out[pl.ds(q, 256, stride=5), :] = flat[pl.ds(q, 256, stride=4), :]
        low = iota((16, 128), 1) < 8
        above, below = edge_total[0:16, :], edge_total[16:32, :]
        for t in range(16):
            left = pltpu.roll(above, (128 - 8 * t) % 128, axis=1)
            right = pltpu.roll(below, (136 - 8 * t) % 128, axis=1)
            out[pl.ds(80 * t + 4, 16, stride=5), :] = jnp.where(low, left, right)


def second_solve_kernel(
    pos,
    intercept,
    received,
    before,
    rest,
    mu_p,
    mu_q,
    w_p,
    w_q,
    gt_hi,
    gt_lo,
    g_hi,
    g_lo,
    out,
    x_hi,
    x_lo,
    update,
    total,
):
    step = pl.program_id(0)

    @pl.when(step == 0)
    def _():
        for j in range(8):
            tiles = block_swap(received[:, j])
            hi, lo = split(tiles.reshape(128, 128))
            x_hi[:, j * 128 : (j + 1) * 128] = hi
            x_lo[:, j * 128 : (j + 1) * 128] = lo

    modes = dot3((x_hi[...], x_lo[...]), (gt_hi[...], gt_lo[...])) + rest[...]
    rho = damping(intercept, mu_p, mu_q)

    def force(tile):
        return modes[tile * 8 : tile * 8 + 8]

    def store(tile, u):
        rows = slice(tile * 8, tile * 8 + 8)
        update[rows, :] = u + before[rows, :]

    cyclic_solve(force, rho, store)
    u = weighted(update, w_p, w_q)
    accumulate(step, total, dot3(u, (g_hi[...], g_lo[...])))

    @pl.when(step == SIZE // P_BLOCK - 1)
    def _():
        for j in range(8):
            tiles = total[:, j * 128 : (j + 1) * 128].reshape(16, 8, 128)
            out[:, j] = block_swap(tiles)


def final_kernel(received, g_hi, g_lo, initial, out):
    rows = split(received[...].T)
    update = dot3(rows, (g_hi[...], g_lo[...]))
    start = initial[...]
    out[0] = update[:STRIP] + start
    out[1] = update[STRIP:] + start


def divergence_kernel(
    pos,
    labels,
    intercept,
    sensitivity,
    received,
    initial,
    near,
    table_hi,
    table_lo,
    out,
    d_ref,
):
    r = pos[1]
    edge_rows = received[pl.ds(4, 256, stride=5), :].T[:16]
    owner = iota((16, 256), 0) % 4
    update = jnp.zeros((144, SIZE), F32)
    for q in range(4):
        inner = received[pl.ds(q, 256, stride=5), :].T
        masked = jnp.where(owner == q, edge_rows, 0.0)
        rows = split(jnp.concatenate([inner, masked], 0))
        update = update + dot3(rows, (table_hi[q], table_lo[q]))
    values = (intercept, sensitivity)
    first = r * STRIP
    own = material_rows(labels, values, first // TILE)
    above = material_rows(labels, values, jnp.maximum(first - 1, 0) // TILE)
    below = material_rows(labels, values, jnp.minimum(first + STRIP, SIZE - 1) // TILE)
    start = initial[...]
    for n in range(2):
        w = update[n * STRIP : (n + 1) * STRIP] + start
        k = conductivity(w, *own)
        at = 128 + 4 * n
        w_above = near[0:1, :] + jnp.sum(update[at : at + 4], 0, keepdims=True)
        w_below = near[1:2, :] + jnp.sum(update[at + 8 : at + 12], 0, keepdims=True)
        k_above = conductivity(w_above, *above)
        k_below = conductivity(w_below, *below)
        enter = 0.5 * (k_above + k[:1]) * (w[:1] - w_above)
        leave = 0.5 * (k_below + k[STRIP - 1 :]) * (w_below - w[STRIP - 1 :])
        enter = jnp.where(r == 0, 0.0, enter)
        leave = jnp.where(r == SIZE // STRIP - 1, 0.0, leave)
        d_ref[n * STRIP : (n + 1) * STRIP, :] = inner_divergence(w, k, enter, leave)
    d = split(d_ref[...])
    for q in range(4):
        modes = dot3((table_hi[q], table_lo[q]), d, dot_nt)
        out[pl.ds(q, 256, stride=4), :] = modes


def whole(shape):
    return pl.BlockSpec(shape, lambda i, *_: (0,) * len(shape))


SMEM = pl.BlockSpec(memory_space=pltpu.SMEM)


def call(kernel, pos, grid, in_specs, out_specs, out_shape, scratch, *args):
    spec = pltpu.PrefetchScalarGridSpec(
        num_scalar_prefetch=1,
        grid=(grid,),
        in_specs=in_specs,
        out_specs=out_specs,
        scratch_shapes=scratch,
    )
    return pl.pallas_call(
        kernel,
        grid_spec=spec,
        out_shape=out_shape,
        compiler_params=pltpu.CompilerParams(vmem_limit_bytes=VMEM_LIMIT),
    )(pos, *args)


def own_block(rows):
    return pl.BlockSpec((None, rows, 128), lambda i, pos: (pos[2], 0, 0))


def exchange(tiles):
    return lax.all_to_all(tiles, BOTH, split_axis=0, concat_axis=0, tiled=True)


def shape_of(*dims):
    return jax.ShapeDtypeStruct(dims, F32)


def shards(
    initial_warmth,
    pattern_choice,
    dissipation_tables,
    material_label,
    intercept_kappa,
    sensitivity_coef,
):
    made = constants()
    t, r = lax.axis_index("tm"), lax.axis_index("rows")
    rows_count = lax.axis_size("rows")
    pos = jnp.stack([t, r, t * rows_count + r]).astype(jnp.int32)
    g, gt = made["g"], made["gt"]
    material = (material_label, intercept_kappa, sensitivity_coef)
    by_mode = pl.BlockSpec((None, 256, SIZE), lambda i, pos: (lax.rem(pos[0], 4), 0, 0))
    started = call(
        start_kernel,
        pos,
        1,
        [SMEM] * 4 + [whole((STRIP, SIZE)), by_mode, by_mode],
        whole((512, 128)),
        shape_of(512, 128),
        [],
        *material,
        pattern_choice.reshape(16, 8),
        initial_warmth,
        *made["by_mode"],
    )
    received = exchange(started.reshape(256, 2, 128)).reshape(512, 128)

    p_row = pl.BlockSpec((1, P_BLOCK), lambda i, pos: (0, i))
    p_block = pl.BlockSpec((128, P_BLOCK), lambda i, pos: (0, i))
    gt_block = pl.BlockSpec((SIZE, P_BLOCK), lambda i, pos: (0, i))
    g_block = pl.BlockSpec((P_BLOCK, SIZE), lambda i, pos: (i, 0))
    spectral = [p_row, own_block(8), p_row, own_block(8), gt_block, gt_block, g_block, g_block]
    spectral_args = (made["mu_p"], made["mu_q"], made["w_p"], made["w_q"], *gt, *g)
    steps = SIZE // P_BLOCK
    edge_block = pl.BlockSpec((32, P_BLOCK), lambda i, pos: (0, i))
    sent, before, rest, near = call(
        first_solve_kernel,
        pos,
        steps,
        [SMEM] * 3
        + [
            whole((512, 128)),
            whole((SIZE, 128)),
            own_block(32),
            own_block(32),
            edge_block,
            edge_block,
            whole((1152, 256)),
            whole((1152, 128)),
            *spectral,
        ],
        [whole((1280, 128)), p_block, p_block, whole((8, SIZE))],
        [shape_of(1280, 128), shape_of(128, SIZE), shape_of(128, SIZE), shape_of(8, SIZE)],
        [
            pltpu.VMEM((144, SIZE), BF16),
            pltpu.VMEM((144, SIZE), BF16),
            pltpu.VMEM((128, SIZE), F32),
            pltpu.VMEM((32, 128), F32),
            pltpu.VMEM((16, 8, 8, 128), F32),
            pltpu.VMEM((16, SIZE), F32),
            pltpu.VMEM((16, SIZE), F32),
        ],
        *material,
        received,
        dissipation_tables.reshape(SIZE, 128),
        *made["own"],
        *made["edge"],
        made["pick"],
        made["spread"],
        *spectral_args,
    )
    received = exchange(sent.reshape(256,1,640)).reshape(1280, 128)
    table = whole((4, 256, SIZE))
    sent = call(
        divergence_kernel,
        pos,
        1,
        [SMEM] * 3 + [whole((1280, 128)), whole((STRIP, SIZE)), whole((8, SIZE)), table, table],
        whole((SIZE, 128)),
        shape_of(SIZE, 128),
        [pltpu.VMEM((128, SIZE), F32)],
        *material,
        received,
        initial_warmth,
        near,
        *made["by_mode"],
    )
    received = exchange(sent.reshape(256, 4, 128)).reshape(16, 8, 8, 128)
    sent = call(
        second_solve_kernel,
        pos,
        steps,
        [SMEM, whole((16, 8, 8, 128)), p_block, p_block, *spectral],
        whole((16, 8, 8, 128)),
        shape_of(16, 8, 8, 128),
        [
            pltpu.VMEM((128, SIZE), BF16),
            pltpu.VMEM((128, SIZE), BF16),
            pltpu.VMEM((128, P_BLOCK), F32),
            pltpu.VMEM((128, SIZE), F32),
        ],
        intercept_kappa,
        received,
        before,
        rest,
        *spectral_args,
    )
    received = exchange(sent.reshape(256, 4, 128)).reshape(SIZE, 128)
    return pl.pallas_call(
        final_kernel,
        grid=(1,),
        in_specs=[whole((SIZE, 128)), whole((SIZE, SIZE)), whole((SIZE, SIZE)), whole((STRIP, SIZE))],
        out_specs=whole((2, STRIP, SIZE)),
        out_shape=shape_of(2, STRIP, SIZE),
        compiler_params=pltpu.CompilerParams(vmem_limit_bytes=VMEM_LIMIT),
    )(received, *g, initial_warmth)


def solution(mesh):
    in_specs = (P("rows", None), P("tm", None, None), P(), P(), P(), P())
    out_specs = P("tm", "rows", None)
    return jax.shard_map(shards, mesh=mesh, in_specs=in_specs, out_specs=out_specs, check_vma=False)
```

```python
import functools
import math

import jax
import jax.numpy as jnp
import ml_dtypes
import numpy as np
from jax import lax
from jax.experimental import pallas as pl
from jax.experimental.pallas import tpu as pltpu
from jax.sharding import PartitionSpec as P

TILE = 128
SIZE = 1024
STEPS = 32
STRIP = 64
DEVICES = 256
ALPHA = 0.05
CROSS_WEIGHT = 1.0 / 64.0
P_BLOCK = 256
BOTH = ("tm", "rows")
F32 = jnp.float32
BF16 = jnp.bfloat16
VMEM_LIMIT = 24 * 1024 * 1024
START_LIMIT = 56 * 1024 * 1024


def halves(table):
    high = table.astype(ml_dtypes.bfloat16)
    low = (table - high.astype(np.float64)).astype(ml_dtypes.bfloat16)
    return high, low


@functools.cache
def constants():
    k = np.arange(SIZE, dtype=np.int64)
    phase = k[:, None] * (2 * k[None, :] + 1) % (4 * SIZE)
    cosines = np.cos(phase.astype(np.float64) * (math.pi / (2 * SIZE)))
    made = {}
    order = np.arange(SIZE).reshape(DEVICES, 4).T.reshape(-1)
    made["table"] = halves(cosines[order].reshape(4, DEVICES, SIZE))
    edge_rows = np.concatenate([np.arange(-1, SIZE - 1, STRIP), np.arange(STRIP, SIZE + 1, STRIP)])
    inside = (edge_rows >= 0) & (edge_rows < SIZE)
    edges = cosines.T[np.clip(edge_rows, 0, SIZE - 1)] * inside[:, None]
    made["edges"] = np.concatenate(halves(edges[:, order]), 0)
    scales = np.zeros((8, SIZE), np.float32)
    scales[0] = (2.0 - 2.0 * np.cos(np.arange(SIZE) * (math.pi / SIZE)))[order]
    scales[1] = 2.0 / SIZE
    scales[1, 0] = 1.0 / SIZE
    made["scales"] = scales
    place = np.zeros((8, 144, 384), np.float32)
    for ty in range(8):
        for row in range(128):
            place[ty, row, (row // 4) * 8 + ty] = 1.0
        for row in range(128, 144):
            for half in range(2):
                place[ty, row, 256 + half * 64 + (row % 4) * 16 + 2 * ty + half] = 1.0
    made["place"] = place.reshape(1152, 384).astype(ml_dtypes.bfloat16)
    return made


def split(values):
    high = values.astype(BF16)
    return high, (values - high.astype(F32)).astype(BF16)


def stacked(values):
    return jnp.concatenate(split(values), 0)


def dot(a, b):
    return jnp.dot(a, b, preferred_element_type=F32)


def dot_nt(a, b):
    return lax.dot_general(a, b, (((1,), (1,)), ((), ())), preferred_element_type=F32)


def rows_by_table(both, high, low, product):
    count = both.shape[0] // 2
    wide = product(both, high)
    return wide[:count] + wide[count:] + product(both[:count], low)


def table_by_rows(high, low, both):
    count = both.shape[0] // 2
    wide = dot_nt(high, both)
    return wide[:, :count] + wide[:, count:] + dot_nt(low, both[:count])


def iota(shape, dim):
    return lax.broadcasted_iota(jnp.int32, shape, dim)


def block_swap(tiles):
    shape = tiles.shape
    swapped = pltpu.roll(pltpu.roll(tiles, 4, axis=1), 64, axis=2)
    diagonal = (iota(shape, 1) < 4) == (iota(shape, 2) < 64)
    return jnp.where(diagonal, tiles, swapped)


def material_row(labels, values, ty):
    return jnp.concatenate(
        [jnp.full((1, TILE), values[labels[ty, tx]], F32) for tx in range(8)], 1
    )


def conductivity(values, base, slope):
    return base * (1.0 + slope * jnp.tanh(values))


def inner_divergence(w, k, above=None, below=None):
    shape = w.shape
    row, column = iota(shape, 0), iota(shape, 1)
    w_next = pltpu.roll(w, STRIP - 1, axis=0)
    k_next = pltpu.roll(k, STRIP - 1, axis=0)
    below = jnp.zeros((1, 1), F32) if below is None else below
    above = jnp.zeros((1, 1), F32) if above is None else above
    down = jnp.where(row == STRIP - 1, below, 0.5 * (k + k_next) * (w_next - w))
    up = jnp.where(row == 0, above, pltpu.roll(down, 1, axis=0))
    w_right = pltpu.roll(w, SIZE - 1, axis=1)
    k_right = pltpu.roll(k, SIZE - 1, axis=1)
    side = CROSS_WEIGHT * (0.5 * (k + k_right) * (w_right - w))
    side = jnp.where(column == SIZE - 1, 0.0, side)
    return down - up + (side - pltpu.roll(side, 1, axis=1))


def material_rows(labels, values, ty):
    return material_row(labels, values[0], ty), material_row(labels, values[1], ty)


def start_kernel(
    pos, labels, intercept, sensitivity, patterns, w_ref, table_hi, table_lo, out
):
    t, r = pos[0], pos[1]
    w = w_ref[...]
    base, slope = material_rows(labels, (intercept, sensitivity), r * STRIP // TILE)
    d = inner_divergence(w, conductivity(w, base, slope))
    padded = jnp.concatenate([jnp.zeros_like(d), d], 0)
    modes = table_by_rows(table_hi[...], table_lo[...], stacked(padded))
    lane = iota((1, 128), 1)
    chosen = jnp.zeros((1, 128), jnp.int32)
    for tx in range(8):
        chosen = jnp.where(lane % 8 == tx, patterns[r, tx], chosen)
    one_hot = jnp.where((chosen == lane // 8) & (lane < 64), 1.0, 0.0).astype(F32)
    out[pl.ds(0, 256, stride=2), :] = modes + one_hot
    columns = pl.ds(pl.multiple_of(t // 2 * 128, 128), 128)
    first, last = w_ref[0:1, columns], w_ref[STRIP - 1 : STRIP, columns]
    first = jnp.where(t % 2 == 0, first, pltpu.roll(first, 64, axis=1))
    last = jnp.where(t % 2 == 0, pltpu.roll(last, 64, axis=1), last)
    edges = jnp.where(lane < 64, first, last)
    out[pl.ds(1, 256, stride=2), :] = jnp.broadcast_to(edges, (256, 128))


def face_fluxes(got, labels, intercept, sensitivity, own, first_ref, last_ref):
    lane = iota((16, 128), 1) < 64
    row = iota((16, 128), 0)
    totals = [jnp.zeros((16, 128), F32)] * 4
    for tx in range(8):
        columns = slice(tx * 128, tx * 128 + 128)
        left = got[tx * 32 : tx * 32 + 16]
        right = got[tx * 32 + 16 : tx * 32 + 32]
        first = jnp.where(lane, left, pltpu.roll(right, 64, axis=1))
        last = jnp.where(lane, pltpu.roll(left, 64, axis=1), right)
        first_ref[:, columns] = first
        last_ref[:, columns] = last
        base = jnp.zeros((16, 128), F32)
        slope = jnp.zeros((16, 128), F32)
        for ty in range(8):
            here = row // 2 == ty
            base = jnp.where(here, intercept[labels[ty, tx]], base)
            slope = jnp.where(here, sensitivity[labels[ty, tx]], slope)
        k_first = conductivity(first, base, slope)
        k_last = conductivity(last, base, slope)
        w_next = pltpu.roll(first, 15, axis=0)
        k_next = pltpu.roll(k_first, 15, axis=0)
        flux = jnp.where(row == 15, 0.0, 0.5 * (k_last + k_next) * (w_next - last))
        for q in range(4):
            totals[q] = totals[q] + own[q * 8 + tx : q * 8 + tx + 1, :] * flux
    sums = [jnp.sum(total, axis=1, keepdims=True) for total in totals]
    down = jnp.concatenate(sums, 0)
    up = jnp.concatenate([pltpu.roll(jnp.broadcast_to(x, (16, 128)), 1, axis=0) for x in sums], 0)
    return down, up[:, :1]


def cyclic_solve(force, rho, store):
    even = iota(rho.shape, 0) < 4
    twice = 2.0 * rho
    square = rho * rho
    drives = [twice * force(tile) for tile in range(STEPS // 2)]
    pairs = [rho * pltpu.roll(drive, 4, axis=0) + drive for drive in drives]
    z = pairs[0]
    for pair in pairs[1:]:
        z = square * z + pair
    power = square
    for _ in range(4):
        power = power * power
    odd = ALPHA * z / (1.0 - ALPHA * power)
    for tile in range(STEPS // 2):
        before = rho * pltpu.roll(odd, 4, axis=0) + drives[tile]
        odd = square * odd + pairs[tile]
        store(tile, jnp.where(even, before, odd))


def own_factors(intercept, scales, device):
    count = intercept.shape[0]
    conduct = intercept[0]
    for region in range(1, count):
        conduct = conduct + intercept[region]
    conduct = conduct / count
    lane = iota((1, SIZE), 1)
    row = iota((8, 128), 0) % 4
    mu = jnp.zeros((8, 128), F32)
    for q in range(4):
        chosen = jnp.where(lane == q * DEVICES + device, scales[0:1, :], 0.0)
        mu = jnp.where(row == q, jnp.sum(chosen, 1, keepdims=True), mu)
    first = (row == 0) & (device == 0)
    weight = jnp.where(first, 1.0 / SIZE, 2.0 / SIZE)
    return conduct, mu[:, :1], weight[:, :1]


def damping(conduct, mu_p, mu_q):
    return 1.0 / (1.0 + 2.0 * (conduct * (mu_p + CROSS_WEIGHT * mu_q)))


def weighted(tiles, scale):
    return stacked(jnp.concatenate([tile * scale for tile in tiles], 0))


def swap_rows(total, rows):
    for j in range(8):
        tiles = total[:, j * 128 : (j + 1) * 128].reshape(16, 8, 128)
        rows[:, j] = block_swap(tiles)


def first_solve_kernel(
    pos,
    labels,
    intercept,
    sensitivity,
    received,
    tables,
    edge_table,
    place,
    scales,
    table_hi,
    table_lo,
    out,
    update,
    rest,
    near,
    x_ref,
    rows,
    first_ref,
    last_ref,
):
    r, device = pos[1], pos[2]
    got = received[pl.ds(0, 256, stride=2), :]
    edges = received[pl.ds(1, 256, stride=2), :]
    group = pl.ds(pl.multiple_of(device // 16 * 16, 16), 16)
    mine = iota((16, SIZE), 0) == device % 16
    pieces = []
    for q in range(4):
        near_rows = table_hi[q, group, :].astype(F32) + table_lo[q, group, :].astype(F32)
        row = jnp.sum(jnp.where(mine, near_rows, 0.0), 0, keepdims=True)
        pieces += [row[:, tx * 128 : (tx + 1) * 128] for tx in range(8)]
    own = jnp.concatenate(pieces, 0)
    down, up = face_fluxes(edges, labels, intercept, sensitivity, own, first_ref, last_ref)
    strip = iota((16, SIZE), 0)
    near[0:1, :] = jnp.sum(jnp.where(strip == r - 1, last_ref[...], 0.0), 0, keepdims=True)
    near[1:2, :] = jnp.sum(jnp.where(strip == r + 1, first_ref[...], 0.0), 0, keepdims=True)
    near[2:8, :] = jnp.zeros((6, SIZE), F32)
    lane = iota((256, 128), 1)
    rolled = pltpu.roll(got, 64, axis=1)
    doubled = jnp.where(lane < 64, got, rolled).astype(BF16)
    chosen = dot(place[:, :256], jnp.concatenate([doubled, doubled], 1))
    match = (iota((1152, 256), 0) % 4) == (iota((1152, 256), 1) // 64)
    chosen = jnp.where(match, chosen, 0.0).astype(BF16)
    by_tile = rows_by_table(stacked(own), *split(tables[...]), dot_nt)
    pieces = [
        by_tile[q * 8 : (q + 1) * 8, k * 128 : (k + 1) * 128] for q in range(4) for k in range(8)
    ]
    a_hi, a_lo = split(jnp.concatenate(pieces, 0))
    few = lane[:64]
    inner = got[:64]
    inner = inner + jnp.where(few == 127, down, 0.0) - jnp.where(few == 64, up, 0.0)
    top = jnp.where(few < 64, pltpu.roll(inner, 64, axis=1), 0.0)
    bottom = jnp.where(few < 64, 0.0, inner)
    d_hi, d_lo = split(jnp.concatenate([top, bottom], 0))
    spread = place[:, 256:]
    both = dot(chosen, a_hi) + dot(chosen, a_lo) + (dot(spread, d_hi) + dot(spread, d_lo))
    for ty in range(8):
        x_ref[:, ty * 128 : (ty + 1) * 128] = stacked(both[ty * 144 : (ty + 1) * 144])

    conduct, mu_q, w_q = own_factors(intercept, scales, device)
    even = iota((8, P_BLOCK), 0) < 4
    total = jnp.zeros((128, SIZE), F32)
    edge_total = jnp.zeros((32, 128), F32)
    for block in range(4):
        lanes = slice(block * P_BLOCK, (block + 1) * P_BLOCK)
        high, low = table_hi[block], table_lo[block]
        modes = rows_by_table(x_ref[...], high, low, dot_nt)
        shared = modes[128:136]
        rho = damping(conduct, scales[0:1, lanes], mu_q)
        last = [jnp.zeros_like(rho)]
        tiles = []

        def force(tile):
            return modes[tile * 8 : tile * 8 + 8] + shared

        def store(tile, u):
            at = slice(tile * 8, tile * 8 + 8)
            update[at, lanes] = u
            turned = pltpu.roll(u, 4, axis=0)
            earlier = jnp.where(even, last[0], turned)
            rest[at, lanes] = modes[at] - 0.5 * (u - earlier)
            last[0] = turned
            tiles.append(u)

        cyclic_solve(force, rho, store)
        u = weighted(tiles, scales[1:2, lanes] * w_q)
        total = total + rows_by_table(u, high, low, dot)
        edge_total = edge_total + table_by_rows(edge_table[:32, lanes], edge_table[32:, lanes], u)

    swap_rows(total, rows)
    flat = rows.reshape(SIZE, 128)
    for q in range(4):
        out[pl.ds(q, 256, stride=5), :] = flat[pl.ds(q, 256, stride=4), :]
    low_lane = iota((16, 128), 1) < 8
    above, below = edge_total[0:16, :], edge_total[16:32, :]
    for t in range(16):
        left = pltpu.roll(above, (128 - 8 * t) % 128, axis=1)
        right = pltpu.roll(below, (136 - 8 * t) % 128, axis=1)
        out[pl.ds(80 * t + 4, 16, stride=5), :] = jnp.where(low_lane, left, right)


def second_solve_kernel(
    pos, intercept, received, before, rest, scales, table_hi, table_lo, out, x_ref
):
    for j in range(8):
        tiles = block_swap(received[:, j])
        x_ref[:, j * 128 : (j + 1) * 128] = stacked(tiles.reshape(128, 128))
    conduct, mu_q, w_q = own_factors(intercept, scales, pos[2])
    total = jnp.zeros((128, SIZE), F32)
    for block in range(4):
        lanes = slice(block * P_BLOCK, (block + 1) * P_BLOCK)
        high, low = table_hi[block], table_lo[block]
        modes = rows_by_table(x_ref[...], high, low, dot_nt) + rest[:, lanes]
        rho = damping(conduct, scales[0:1, lanes], mu_q)
        tiles = []

        def force(tile):
            return modes[tile * 8 : tile * 8 + 8]

        def store(tile, u):
            tiles.append(u + before[tile * 8 : tile * 8 + 8, lanes])

        cyclic_solve(force, rho, store)
        u = weighted(tiles, scales[1:2, lanes] * w_q)
        total = total + rows_by_table(u, high, low, dot)
    swap_rows(total, out)


def final_kernel(received, table_hi, table_lo, initial, out):
    update = jnp.zeros((128, SIZE), F32)
    for q in range(4):
        rows = stacked(received[pl.ds(q, 256, stride=4), :].T)
        update = update + rows_by_table(rows, table_hi[q], table_lo[q], dot)
    start = initial[...]
    out[0] = update[:STRIP] + start
    out[1] = update[STRIP:] + start


def divergence_kernel(
    pos,
    labels,
    intercept,
    sensitivity,
    received,
    initial,
    near,
    table_hi,
    table_lo,
    out,
    d_ref,
):
    r = pos[1]
    edge_rows = received[pl.ds(4, 256, stride=5), :].T[:16]
    owner = iota((16, 256), 0) % 4
    update = jnp.zeros((144, SIZE), F32)
    for q in range(4):
        inner = received[pl.ds(q, 256, stride=5), :].T
        masked = jnp.where(owner == q, edge_rows, 0.0)
        rows = stacked(jnp.concatenate([inner, masked], 0))
        update = update + rows_by_table(rows, table_hi[q], table_lo[q], dot)
    values = (intercept, sensitivity)
    first = r * STRIP
    own = material_rows(labels, values, first // TILE)
    above = material_rows(labels, values, jnp.maximum(first - 1, 0) // TILE)
    below = material_rows(labels, values, jnp.minimum(first + STRIP, SIZE - 1) // TILE)
    start = initial[...]
    for n in range(2):
        w = update[n * STRIP : (n + 1) * STRIP] + start
        k = conductivity(w, *own)
        at = 128 + 4 * n
        w_above = near[0:1, :] + jnp.sum(update[at : at + 4], 0, keepdims=True)
        w_below = near[1:2, :] + jnp.sum(update[at + 8 : at + 12], 0, keepdims=True)
        k_above = conductivity(w_above, *above)
        k_below = conductivity(w_below, *below)
        enter = 0.5 * (k_above + k[:1]) * (w[:1] - w_above)
        leave = 0.5 * (k_below + k[STRIP - 1 :]) * (w_below - w[STRIP - 1 :])
        enter = jnp.where(r == 0, 0.0, enter)
        leave = jnp.where(r == SIZE // STRIP - 1, 0.0, leave)
        d_ref[n * STRIP : (n + 1) * STRIP, :] = inner_divergence(w, k, enter, leave)
    d = stacked(d_ref[...])
    for q in range(4):
        out[pl.ds(q, 256, stride=4), :] = table_by_rows(table_hi[q], table_lo[q], d)


def whole(shape):
    return pl.BlockSpec(shape, lambda i, *_: (0,) * len(shape))


SMEM = pl.BlockSpec(memory_space=pltpu.SMEM)


def call(kernel, pos, limit, in_specs, outs, scratch, *args):
    spec = pltpu.PrefetchScalarGridSpec(
        num_scalar_prefetch=1,
        grid=(1,),
        in_specs=in_specs,
        out_specs=[whole(out) for out in outs],
        scratch_shapes=scratch,
    )
    results = pl.pallas_call(
        kernel,
        grid_spec=spec,
        out_shape=[jax.ShapeDtypeStruct(out, F32) for out in outs],
        compiler_params=pltpu.CompilerParams(vmem_limit_bytes=limit),
    )(pos, *args)
    return results if len(outs) > 1 else results[0]


def exchange(tiles, width):
    shape = (DEVICES, width // 128, 128) if width in (256, 512) else (DEVICES, 1, width)
    moved = lax.all_to_all(tiles.reshape(shape), BOTH, split_axis=0, concat_axis=0, tiled=True)
    return moved.reshape(-1, 128)


def shards(
    initial_warmth,
    pattern_choice,
    dissipation_tables,
    material_label,
    intercept_kappa,
    sensitivity_coef,
):
    made = constants()
    t, r = lax.axis_index("tm"), lax.axis_index("rows")
    pos = jnp.stack([t, r, t * lax.axis_size("rows") + r]).astype(jnp.int32)
    material = (material_label, intercept_kappa, sensitivity_coef)
    table = made["table"]
    one_number = pl.BlockSpec((None, 256, SIZE), lambda i, pos: (lax.rem(pos[0], 4), 0, 0))
    tables = [whole((4, 256, SIZE))] * 2
    strip = whole((STRIP, SIZE))
    field = whole((128, SIZE))
    few = whole((8, SIZE))
    sent = call(
        start_kernel,
        pos,
        START_LIMIT,
        [SMEM] * 4 + [strip, one_number, one_number],
        [(512, 128)],
        [],
        *material,
        pattern_choice.reshape(16, 8),
        initial_warmth,
        *table,
    )
    received = exchange(sent, 256)
    sent, before, rest, near = call(
        first_solve_kernel,
        pos,
        VMEM_LIMIT,
        [SMEM] * 3
        + [
            whole((512, 128)),
            whole((SIZE, 128)),
            whole((64, SIZE)),
            whole((1152, 384)),
            few,
            *tables,
        ],
        [(1280, 128), (128, SIZE), (128, SIZE), (8, SIZE)],
        [
            pltpu.VMEM((288, SIZE), BF16),
            pltpu.VMEM((16, 8, 8, 128), F32),
            pltpu.VMEM((16, SIZE), F32),
            pltpu.VMEM((16, SIZE), F32),
        ],
        *material,
        received,
        dissipation_tables.reshape(SIZE, 128),
        made["edges"],
        made["place"],
        made["scales"],
        *table,
    )
    received = exchange(sent, 640)
    sent = call(
        divergence_kernel,
        pos,
        VMEM_LIMIT,
        [SMEM] * 3 + [whole((1280, 128)), strip, few, *tables],
        [(SIZE, 128)],
        [pltpu.VMEM((128, SIZE), F32)],
        *material,
        received,
        initial_warmth,
        near,
        *table,
    )
    received = exchange(sent, 512)
    sent = call(
        second_solve_kernel,
        pos,
        VMEM_LIMIT,
        [SMEM, whole((16, 8, 8, 128)), field, field, few, *tables],
        [(16, 8, 8, 128)],
        [pltpu.VMEM((256, SIZE), BF16)],
        intercept_kappa,
        received.reshape(16, 8, 8, 128),
        before,
        rest,
        made["scales"],
        *table,
    )
    received = exchange(sent, 512)
    return pl.pallas_call(
        final_kernel,
        grid=(1,),
        in_specs=[whole((SIZE, 128)), *tables, strip],
        out_specs=whole((2, STRIP, SIZE)),
        out_shape=jax.ShapeDtypeStruct((2, STRIP, SIZE), F32),
        compiler_params=pltpu.CompilerParams(vmem_limit_bytes=VMEM_LIMIT),
    )(received, *table, initial_warmth)


def solution(mesh):
    in_specs = (P("rows", None), P("tm", None, None), P(), P(), P(), P())
    out_specs = P("tm", "rows", None)
    return jax.shard_map(shards, mesh=mesh, in_specs=in_specs, out_specs=out_specs, check_vma=False)
```

```python
import functools
import math

import jax
import jax.numpy as jnp
import ml_dtypes
import numpy as np
from jax import lax
from jax.experimental import pallas as pl
from jax.experimental.pallas import tpu as pltpu
from jax.sharding import PartitionSpec as P

TILE = 128
SIZE = 1024
STEPS = 32
STRIP = 64
DEVICES = 256
ALPHA = 0.05
CROSS_WEIGHT = 1.0 / 64.0
P_BLOCK = 256
BOTH = ("tm", "rows")
F32 = jnp.float32
BF16 = jnp.bfloat16
VMEM_LIMIT = 24 * 1024 * 1024
START_LIMIT = 56 * 1024 * 1024


def halves(table):
    high = table.astype(ml_dtypes.bfloat16)
    low = (table - high.astype(np.float64)).astype(ml_dtypes.bfloat16)
    return high, low


@functools.cache
def constants():
    k = np.arange(SIZE, dtype=np.int64)
    phase = k[:, None] * (2 * k[None, :] + 1) % (4 * SIZE)
    cosines = np.cos(phase.astype(np.float64) * (math.pi / (2 * SIZE)))
    made = {}
    order = np.arange(SIZE).reshape(DEVICES, 4).T.reshape(-1)
    made["table"] = halves(cosines[order].reshape(4, DEVICES, SIZE))
    edge_rows = np.concatenate([np.arange(-1, SIZE - 1, STRIP), np.arange(STRIP, SIZE + 1, STRIP)])
    inside = (edge_rows >= 0) & (edge_rows < SIZE)
    edges = cosines.T[np.clip(edge_rows, 0, SIZE - 1)] * inside[:, None]
    made["edges"] = np.concatenate(halves(edges[:, order]), 0)
    scales = np.zeros((8, SIZE), np.float32)
    scales[0] = (2.0 - 2.0 * np.cos(np.arange(SIZE) * (math.pi / SIZE)))[order]
    scales[1] = 2.0 / SIZE
    scales[1, 0] = 1.0 / SIZE
    made["scales"] = scales
    return made


def split(values):
    high = values.astype(BF16)
    return high, (values - high.astype(F32)).astype(BF16)


def stacked(values):
    return jnp.concatenate(split(values), 0)


def dot(a, b):
    return jnp.dot(a, b, preferred_element_type=F32)


def dot_nt(a, b):
    return lax.dot_general(a, b, (((1,), (1,)), ((), ())), preferred_element_type=F32)


def rows_by_table(both, high, low, product):
    count = both.shape[0] // 2
    wide = product(both, high)
    return wide[:count] + wide[count:] + product(both[:count], low)


def table_by_rows(high, low, both):
    count = both.shape[0] // 2
    wide = dot_nt(high, both)
    return wide[:, :count] + wide[:, count:] + dot_nt(low, both[:count])


def iota(shape, dim):
    return lax.broadcasted_iota(jnp.int32, shape, dim)


def block_swap(tiles):
    shape = tiles.shape
    swapped = pltpu.roll(pltpu.roll(tiles, 4, axis=1), 64, axis=2)
    diagonal = (iota(shape, 1) < 4) == (iota(shape, 2) < 64)
    return jnp.where(diagonal, tiles, swapped)


def material_row(labels, values, ty):
    return jnp.concatenate(
        [jnp.full((1, TILE), values[labels[ty, tx]], F32) for tx in range(8)], 1
    )


def conductivity(values, base, slope):
    return base * (1.0 + slope * jnp.tanh(values))


def inner_divergence(w, k, above=None, below=None):
    shape = w.shape
    row, column = iota(shape, 0), iota(shape, 1)
    w_next = pltpu.roll(w, STRIP - 1, axis=0)
    k_next = pltpu.roll(k, STRIP - 1, axis=0)
    below = jnp.zeros((1, 1), F32) if below is None else below
    above = jnp.zeros((1, 1), F32) if above is None else above
    down = jnp.where(row == STRIP - 1, below, 0.5 * (k + k_next) * (w_next - w))
    up = jnp.where(row == 0, above, pltpu.roll(down, 1, axis=0))
    w_right = pltpu.roll(w, SIZE - 1, axis=1)
    k_right = pltpu.roll(k, SIZE - 1, axis=1)
    side = CROSS_WEIGHT * (0.5 * (k + k_right) * (w_right - w))
    side = jnp.where(column == SIZE - 1, 0.0, side)
    return down - up + (side - pltpu.roll(side, 1, axis=1))


def material_rows(labels, values, ty):
    return material_row(labels, values[0], ty), material_row(labels, values[1], ty)


def position():
    t, r = lax.axis_index("tm"), lax.axis_index("rows")
    return t, r, t * lax.axis_size("rows") + r


def start_kernel(
    labels,
    intercept,
    sensitivity,
    patterns,
    w_ref,
    all_hi,
    all_lo,
    out,
    table_hi,
    table_lo,
    sem,
):
    t, r, _ = position()
    number = lax.rem(t, 4)
    fetch_hi = pltpu.make_async_copy(all_hi.at[number], table_hi, sem.at[0])
    fetch_lo = pltpu.make_async_copy(all_lo.at[number], table_lo, sem.at[1])
    fetch_hi.start()
    fetch_lo.start()
    w = w_ref[...]
    base, slope = material_rows(labels, (intercept, sensitivity), r * STRIP // TILE)
    both = stacked(inner_divergence(w, conductivity(w, base, slope)))
    fetch_hi.wait()
    wide = dot_nt(table_hi[...], both)
    fetch_lo.wait()
    rest = dot_nt(table_lo[...], both)
    modes = wide + pltpu.roll(wide + rest, 64, axis=1)
    modes = jnp.where(iota((256, 128), 1) < 64, 0.0, modes)
    lane = iota((1, 128), 1)
    chosen = jnp.zeros((1, 128), jnp.int32)
    for tx in range(8):
        chosen = jnp.where(lane % 8 == tx, patterns[r, tx], chosen)
    one_hot = jnp.where((chosen == lane // 8) & (lane < 64), 1.0, 0.0).astype(F32)
    out[pl.ds(0, 256, stride=2), :] = modes + one_hot
    columns = pl.ds(pl.multiple_of(t // 2 * 128, 128), 128)
    first, last = w_ref[0:1, columns], w_ref[STRIP - 1 : STRIP, columns]
    first = jnp.where(t % 2 == 0, first, pltpu.roll(first, 64, axis=1))
    last = jnp.where(t % 2 == 0, pltpu.roll(last, 64, axis=1), last)
    edges = jnp.where(lane < 64, first, last)
    out[pl.ds(1, 256, stride=2), :] = jnp.broadcast_to(edges, (256, 128))


def face_fluxes(got, labels, intercept, sensitivity, own, first_ref, last_ref):
    lane = iota((16, 128), 1) < 64
    row = iota((16, 128), 0)
    totals = [jnp.zeros((16, 128), F32)] * 4
    for tx in range(8):
        columns = slice(tx * 128, tx * 128 + 128)
        left = got[tx * 32 : tx * 32 + 16]
        right = got[tx * 32 + 16 : tx * 32 + 32]
        first = jnp.where(lane, left, pltpu.roll(right, 64, axis=1))
        last = jnp.where(lane, pltpu.roll(left, 64, axis=1), right)
        first_ref[:, columns] = first
        last_ref[:, columns] = last
        base = jnp.zeros((16, 128), F32)
        slope = jnp.zeros((16, 128), F32)
        for ty in range(8):
            here = row // 2 == ty
            base = jnp.where(here, intercept[labels[ty, tx]], base)
            slope = jnp.where(here, sensitivity[labels[ty, tx]], slope)
        k_first = conductivity(first, base, slope)
        k_last = conductivity(last, base, slope)
        w_next = pltpu.roll(first, 15, axis=0)
        k_next = pltpu.roll(k_first, 15, axis=0)
        flux = jnp.where(row == 15, 0.0, 0.5 * (k_last + k_next) * (w_next - last))
        for q in range(4):
            totals[q] = totals[q] + own[q * 8 + tx : q * 8 + tx + 1, :] * flux
    sums = [jnp.sum(total, axis=1, keepdims=True) for total in totals]
    down = jnp.concatenate(sums, 0)
    up = jnp.concatenate([pltpu.roll(jnp.broadcast_to(x, (16, 128)), 1, axis=0) for x in sums], 0)
    return down, up[:, :1]


def cyclic_solve(force, rho, store):
    even = iota(rho.shape, 0) < 4
    twice = 2.0 * rho
    square = rho * rho
    drives = [twice * force(tile) for tile in range(STEPS // 2)]
    pairs = [rho * pltpu.roll(drive, 4, axis=0) + drive for drive in drives]
    z = pairs[0]
    for pair in pairs[1:]:
        z = square * z + pair
    power = square
    for _ in range(4):
        power = power * power
    odd = ALPHA * z / (1.0 - ALPHA * power)
    for tile in range(STEPS // 2):
        before = rho * pltpu.roll(odd, 4, axis=0) + drives[tile]
        odd = square * odd + pairs[tile]
        store(tile, jnp.where(even, before, odd))


def own_factors(intercept, scales, device):
    count = intercept.shape[0]
    conduct = intercept[0]
    for region in range(1, count):
        conduct = conduct + intercept[region]
    conduct = conduct / count
    lane = iota((1, SIZE), 1)
    row = iota((8, 128), 0) % 4
    mu = jnp.zeros((8, 128), F32)
    for q in range(4):
        chosen = jnp.where(lane == q * DEVICES + device, scales[0:1, :], 0.0)
        mu = jnp.where(row == q, jnp.sum(chosen, 1, keepdims=True), mu)
    first = (row == 0) & (device == 0)
    weight = jnp.where(first, 1.0 / SIZE, 2.0 / SIZE)
    return conduct, mu[:, :1], weight[:, :1]


def damping(conduct, mu_p, mu_q):
    return 1.0 / (1.0 + 2.0 * (conduct * (mu_p + CROSS_WEIGHT * mu_q)))


def weighted(tiles, scale):
    return stacked(jnp.concatenate([tile * scale for tile in tiles], 0))


def swap_rows(total, rows):
    for j in range(8):
        tiles = total[:, j * 128 : (j + 1) * 128].reshape(16, 8, 128)
        rows[:, j] = block_swap(tiles)


def first_solve_kernel(
    labels,
    intercept,
    sensitivity,
    received,
    tables,
    edge_table,
    scales,
    table_hi,
    table_lo,
    out,
    update,
    rest,
    near,
    x_ref,
    rows,
    first_ref,
    last_ref,
):
    _, r, device = position()
    edges = received[pl.ds(1, 256, stride=2), :]
    group = pl.ds(pl.multiple_of(device // 16 * 16, 16), 16)
    mine = iota((16, SIZE), 0) == device % 16
    pieces = []
    for q in range(4):
        near_rows = table_hi[q, group, :].astype(F32) + table_lo[q, group, :].astype(F32)
        row = jnp.sum(jnp.where(mine, near_rows, 0.0), 0, keepdims=True)
        pieces += [row[:, tx * 128 : (tx + 1) * 128] for tx in range(8)]
    own = jnp.concatenate(pieces, 0)
    down, up = face_fluxes(edges, labels, intercept, sensitivity, own, first_ref, last_ref)
    strip = iota((16, SIZE), 0)
    near[0:1, :] = jnp.sum(jnp.where(strip == r - 1, last_ref[...], 0.0), 0, keepdims=True)
    near[1:2, :] = jnp.sum(jnp.where(strip == r + 1, first_ref[...], 0.0), 0, keepdims=True)
    near[2:8, :] = jnp.zeros((6, SIZE), F32)
    repeat = (iota((128, 32), 0) // 4 == iota((128, 32), 1)).astype(F32).astype(BF16)
    match = iota((128, 256), 0) % 4 == iota((128, 256), 1) // 64
    chosen = []
    for ty in range(8):
        part = received[pl.ds(2 * ty, 32, stride=16), :]
        part = jnp.where(iota((32, 128), 1) < 64, part, pltpu.roll(part, 64, axis=1)).astype(BF16)
        rows_nq = dot(repeat, jnp.concatenate([part, part], 1))
        chosen.append(jnp.where(match, rows_nq, 0.0).astype(BF16))
    chosen = jnp.concatenate(chosen, 0)
    by_tile = rows_by_table(stacked(own), *split(tables[...]), dot_nt)
    pieces = [
        by_tile[q * 8 : (q + 1) * 8, k * 128 : (k + 1) * 128] for q in range(4) for k in range(8)
    ]
    a_hi, a_lo = split(jnp.concatenate(pieces, 0))
    few = iota((64, 128), 1)
    inner = received[pl.ds(0, 64, stride=2), :]
    inner = inner + jnp.where(few == 127, down, 0.0) - jnp.where(few == 64, up, 0.0)
    top = jnp.where(few < 64, pltpu.roll(inner, 64, axis=1), 0.0)
    bottom = jnp.where(few < 64, 0.0, inner)
    d_hi, d_lo = split(jnp.concatenate([top, bottom], 0))
    to, source = iota((128, 128), 0), iota((128, 128), 1)
    same_mode = to % 4 == source // 16 % 4
    same_strip = source % 16 == 2 * (to // 16) + source // 64
    spread = (same_mode & same_strip).astype(F32).astype(BF16)
    power = dot(chosen, a_hi) + dot(chosen, a_lo)
    start = dot(spread, d_hi) + dot(spread, d_lo)
    for ty in range(8):
        parts = [power[ty * 128 : (ty + 1) * 128], start[ty * 16 : (ty + 1) * 16]]
        x_ref[:, ty * 128 : (ty + 1) * 128] = stacked(jnp.concatenate(parts, 0))

    conduct, mu_q, w_q = own_factors(intercept, scales, device)
    even = iota((8, P_BLOCK), 0) < 4
    total = jnp.zeros((128, SIZE), F32)
    edge_total = jnp.zeros((32, 128), F32)
    for block in range(4):
        lanes = slice(block * P_BLOCK, (block + 1) * P_BLOCK)
        high, low = table_hi[block], table_lo[block]
        modes = rows_by_table(x_ref[...], high, low, dot_nt)
        shared = modes[128:136]
        rho = damping(conduct, scales[0:1, lanes], mu_q)
        last = [jnp.zeros_like(rho)]
        tiles = []

        def force(tile):
            return modes[tile * 8 : tile * 8 + 8] + shared

        def store(tile, u):
            at = slice(tile * 8, tile * 8 + 8)
            update[at, lanes] = u
            turned = pltpu.roll(u, 4, axis=0)
            earlier = jnp.where(even, last[0], turned)
            rest[at, lanes] = modes[at] - 0.5 * (u - earlier)
            last[0] = turned
            tiles.append(u)

        cyclic_solve(force, rho, store)
        u = weighted(tiles, scales[1:2, lanes] * w_q)
        total = total + rows_by_table(u, high, low, dot)
        edge_total = edge_total + table_by_rows(edge_table[:32, lanes], edge_table[32:, lanes], u)

    swap_rows(total, rows)
    flat = rows.reshape(SIZE, 128)
    for q in range(4):
        out[pl.ds(q, 256, stride=5), :] = flat[pl.ds(q, 256, stride=4), :]
    low_lane = iota((16, 128), 1) < 8
    above, below = edge_total[0:16, :], edge_total[16:32, :]
    for t in range(16):
        left = pltpu.roll(above, (128 - 8 * t) % 128, axis=1)
        right = pltpu.roll(below, (136 - 8 * t) % 128, axis=1)
        out[pl.ds(80 * t + 4, 16, stride=5), :] = jnp.where(low_lane, left, right)


def second_solve_kernel(
    intercept, received, before, rest, scales, table_hi, table_lo, out, x_ref
):
    for j in range(8):
        tiles = block_swap(received[:, j])
        x_ref[:, j * 128 : (j + 1) * 128] = stacked(tiles.reshape(128, 128))
    conduct, mu_q, w_q = own_factors(intercept, scales, position()[2])
    total = jnp.zeros((128, SIZE), F32)
    for block in range(4):
        lanes = slice(block * P_BLOCK, (block + 1) * P_BLOCK)
        high, low = table_hi[block], table_lo[block]
        modes = rows_by_table(x_ref[...], high, low, dot_nt) + rest[:, lanes]
        rho = damping(conduct, scales[0:1, lanes], mu_q)
        tiles = []

        def force(tile):
            return modes[tile * 8 : tile * 8 + 8]

        def store(tile, u):
            tiles.append(u + before[tile * 8 : tile * 8 + 8, lanes])

        cyclic_solve(force, rho, store)
        u = weighted(tiles, scales[1:2, lanes] * w_q)
        total = total + rows_by_table(u, high, low, dot)
    swap_rows(total, out)


def final_kernel(received, table_hi, table_lo, initial, out):
    update = jnp.zeros((128, SIZE), F32)
    for q in range(4):
        rows = stacked(received[pl.ds(q, 256, stride=4), :].T)
        update = update + rows_by_table(rows, table_hi[q], table_lo[q], dot)
    start = initial[...]
    out[0] = update[:STRIP] + start
    out[1] = update[STRIP:] + start


def divergence_kernel(
    labels,
    intercept,
    sensitivity,
    received,
    initial,
    near,
    table_hi,
    table_lo,
    out,
    d_ref,
):
    _, r, _ = position()
    edge_rows = received[pl.ds(4, 256, stride=5), :].T[:16]
    owner = iota((16, 256), 0) % 4
    update = jnp.zeros((144, SIZE), F32)
    for q in range(4):
        inner = received[pl.ds(q, 256, stride=5), :].T
        masked = jnp.where(owner == q, edge_rows, 0.0)
        rows = stacked(jnp.concatenate([inner, masked], 0))
        update = update + rows_by_table(rows, table_hi[q], table_lo[q], dot)
    values = (intercept, sensitivity)
    first = r * STRIP
    own = material_rows(labels, values, first // TILE)
    above = material_rows(labels, values, jnp.maximum(first - 1, 0) // TILE)
    below = material_rows(labels, values, jnp.minimum(first + STRIP, SIZE - 1) // TILE)
    start = initial[...]
    for n in range(2):
        w = update[n * STRIP : (n + 1) * STRIP] + start
        k = conductivity(w, *own)
        at = 128 + 4 * n
        w_above = near[0:1, :] + jnp.sum(update[at : at + 4], 0, keepdims=True)
        w_below = near[1:2, :] + jnp.sum(update[at + 8 : at + 12], 0, keepdims=True)
        k_above = conductivity(w_above, *above)
        k_below = conductivity(w_below, *below)
        enter = 0.5 * (k_above + k[:1]) * (w[:1] - w_above)
        leave = 0.5 * (k_below + k[STRIP - 1 :]) * (w_below - w[STRIP - 1 :])
        enter = jnp.where(r == 0, 0.0, enter)
        leave = jnp.where(r == SIZE // STRIP - 1, 0.0, leave)
        d_ref[n * STRIP : (n + 1) * STRIP, :] = inner_divergence(w, k, enter, leave)
    d = stacked(d_ref[...])
    for q in range(4):
        out[pl.ds(q, 256, stride=4), :] = table_by_rows(table_hi[q], table_lo[q], d)


def whole(shape):
    return pl.BlockSpec(shape, lambda i: (0,) * len(shape))


SMEM = pl.BlockSpec(memory_space=pltpu.SMEM)
HBM = pl.BlockSpec(memory_space=pltpu.HBM)


def call(kernel, limit, in_specs, outs, scratch, *args):
    results = pl.pallas_call(
        kernel,
        grid=(1,),
        in_specs=in_specs,
        out_specs=[whole(out) for out in outs],
        scratch_shapes=scratch,
        out_shape=[jax.ShapeDtypeStruct(out, F32) for out in outs],
        compiler_params=pltpu.CompilerParams(vmem_limit_bytes=limit),
    )(*args)
    return results if len(outs) > 1 else results[0]


def exchange(tiles, width):
    shape = (DEVICES, width // 128, 128) if width in (256, 512) else (DEVICES, 1, width)
    moved = lax.all_to_all(tiles.reshape(shape), BOTH, split_axis=0, concat_axis=0, tiled=True)
    return moved.reshape(-1, 128)


def shards(
    initial_warmth,
    pattern_choice,
    dissipation_tables,
    material_label,
    intercept_kappa,
    sensitivity_coef,
):
    made = constants()
    material = (material_label, intercept_kappa, sensitivity_coef)
    table = made["table"]
    tables = [whole((4, 256, SIZE))] * 2
    strip = whole((STRIP, SIZE))
    field = whole((128, SIZE))
    few = whole((8, SIZE))
    sent = call(
        start_kernel,
        START_LIMIT,
        [SMEM] * 4 + [strip, HBM, HBM],
        [(512, 128)],
        [
            pltpu.VMEM((256, SIZE), BF16),
            pltpu.VMEM((256, SIZE), BF16),
            pltpu.SemaphoreType.DMA((2,)),
        ],
        *material,
        pattern_choice.reshape(16, 8),
        initial_warmth,
        *table,
    )
    received = exchange(sent, 256)
    sent, before, rest, near = call(
        first_solve_kernel,
        VMEM_LIMIT,
        [SMEM] * 3
        + [
            whole((512, 128)),
            whole((SIZE, 128)),
            whole((64, SIZE)),
            few,
            *tables,
        ],
        [(1280, 128), (128, SIZE), (128, SIZE), (8, SIZE)],
        [
            pltpu.VMEM((288, SIZE), BF16),
            pltpu.VMEM((16, 8, 8, 128), F32),
            pltpu.VMEM((16, SIZE), F32),
            pltpu.VMEM((16, SIZE), F32),
        ],
        *material,
        received,
        dissipation_tables.reshape(SIZE, 128),
        made["edges"],
        made["scales"],
        *table,
    )
    received = exchange(sent, 640)
    sent = call(
        divergence_kernel,
        VMEM_LIMIT,
        [SMEM] * 3 + [whole((1280, 128)), strip, few, *tables],
        [(SIZE, 128)],
        [pltpu.VMEM((128, SIZE), F32)],
        *material,
        received,
        initial_warmth,
        near,
        *table,
    )
    received = exchange(sent, 512)
    sent = call(
        second_solve_kernel,
        VMEM_LIMIT,
        [SMEM, whole((16, 8, 8, 128)), field, field, few, *tables],
        [(16, 8, 8, 128)],
        [pltpu.VMEM((256, SIZE), BF16)],
        intercept_kappa,
        received.reshape(16, 8, 8, 128),
        before,
        rest,
        made["scales"],
        *table,
    )
    received = exchange(sent, 512)
    return call(
        final_kernel,
        VMEM_LIMIT,
        [whole((SIZE, 128)), *tables, strip],
        [(2, STRIP, SIZE)],
        [],
        received,
        *table,
        initial_warmth,
    )


def solution(mesh):
    in_specs = (P("rows", None), P("tm", None, None), P(), P(), P(), P())
    out_specs = P("tm", "rows", None)
    return jax.shard_map(shards, mesh=mesh, in_specs=in_specs, out_specs=out_specs, check_vma=False)
```

```python
import functools
import math

import jax
import jax.numpy as jnp
import ml_dtypes
import numpy as np
from jax import lax
from jax.experimental import pallas as pl
from jax.experimental.pallas import tpu as pltpu
from jax.sharding import PartitionSpec as P

TILE = 128
SIZE = 1024
STEPS = 32
STRIP = 64
DEVICES = 256
ALPHA = 0.05
CROSS_WEIGHT = 1.0 / 64.0
P_BLOCK = 256
BOTH = ("tm", "rows")
F32 = jnp.float32
BF16 = jnp.bfloat16
VMEM_LIMIT = 24 * 1024 * 1024
START_LIMIT = 56 * 1024 * 1024


def halves(table):
    high = table.astype(ml_dtypes.bfloat16)
    low = (table - high.astype(np.float64)).astype(ml_dtypes.bfloat16)
    return high, low


@functools.cache
def constants():
    k = np.arange(SIZE, dtype=np.int64)
    phase = k[:, None] * (2 * k[None, :] + 1) % (4 * SIZE)
    cosines = np.cos(phase.astype(np.float64) * (math.pi / (2 * SIZE)))
    made = {}
    order = np.arange(SIZE).reshape(DEVICES, 4).T.reshape(-1)
    made["table"] = halves(cosines[order].reshape(4, DEVICES, SIZE))
    edge_rows = np.concatenate([np.arange(-1, SIZE - 1, STRIP), np.arange(STRIP, SIZE + 1, STRIP)])
    inside = (edge_rows >= 0) & (edge_rows < SIZE)
    edges = cosines.T[np.clip(edge_rows, 0, SIZE - 1)] * inside[:, None]
    made["edges"] = np.concatenate(halves(edges[:, order]), 0)
    scales = np.zeros((8, SIZE), np.float32)
    scales[0] = (2.0 - 2.0 * np.cos(np.arange(SIZE) * (math.pi / SIZE)))[order]
    scales[1] = 2.0 / SIZE
    scales[1, 0] = 1.0 / SIZE
    made["scales"] = scales
    return made


def split(values):
    high = values.astype(BF16)
    return high, (values - high.astype(F32)).astype(BF16)


def stacked(values):
    return jnp.concatenate(split(values), 0)


def dot(a, b):
    return jnp.dot(a, b, preferred_element_type=F32)


def dot_nt(a, b):
    return lax.dot_general(a, b, (((1,), (1,)), ((), ())), preferred_element_type=F32)


def rows_by_table(both, high, low, product):
    count = both.shape[0] // 2
    wide = product(both, high)
    return wide[:count] + wide[count:] + product(both[:count], low)


def table_by_rows(high, low, both):
    count = both.shape[0] // 2
    wide = dot_nt(high, both)
    return wide[:, :count] + wide[:, count:] + dot_nt(low, both[:count])


def iota(shape, dim):
    return lax.broadcasted_iota(jnp.int32, shape, dim)


def block_swap(tiles):
    shape = tiles.shape
    swapped = pltpu.roll(pltpu.roll(tiles, 4, axis=1), 64, axis=2)
    diagonal = (iota(shape, 1) < 4) == (iota(shape, 2) < 64)
    return jnp.where(diagonal, tiles, swapped)


def material_row(labels, values, ty):
    return jnp.concatenate(
        [jnp.full((1, TILE), values[labels[ty, tx]], F32) for tx in range(8)], 1
    )


def conductivity(values, base, slope):
    return base * (1.0 + slope * jnp.tanh(values))


def inner_divergence(w, k, above=None, below=None):
    shape = w.shape
    row, column = iota(shape, 0), iota(shape, 1)
    w_next = pltpu.roll(w, STRIP - 1, axis=0)
    k_next = pltpu.roll(k, STRIP - 1, axis=0)
    below = jnp.zeros((1, 1), F32) if below is None else below
    above = jnp.zeros((1, 1), F32) if above is None else above
    down = jnp.where(row == STRIP - 1, below, 0.5 * (k + k_next) * (w_next - w))
    up = jnp.where(row == 0, above, pltpu.roll(down, 1, axis=0))
    w_right = pltpu.roll(w, SIZE - 1, axis=1)
    k_right = pltpu.roll(k, SIZE - 1, axis=1)
    side = CROSS_WEIGHT * (0.5 * (k + k_right) * (w_right - w))
    side = jnp.where(column == SIZE - 1, 0.0, side)
    return down - up + (side - pltpu.roll(side, 1, axis=1))


def material_rows(labels, values, ty):
    return material_row(labels, values[0], ty), material_row(labels, values[1], ty)


def position():
    t, r = lax.axis_index("tm"), lax.axis_index("rows")
    return t, r, t * lax.axis_size("rows") + r


def start_kernel(
    labels,
    intercept,
    sensitivity,
    patterns,
    w_ref,
    table_hi,
    table_lo,
    out,
):
    t, r, _ = position()
    w = w_ref[...]
    base, slope = material_rows(labels, (intercept, sensitivity), r * STRIP // TILE)
    both = stacked(inner_divergence(w, conductivity(w, base, slope)))
    wide = dot_nt(table_hi[...], both)
    rest = dot_nt(table_lo[...], both)
    modes = wide + pltpu.roll(wide + rest, 64, axis=1)
    modes = jnp.where(iota((256, 128), 1) < 64, 0.0, modes)
    lane = iota((1, 128), 1)
    chosen = jnp.zeros((1, 128), jnp.int32)
    for tx in range(8):
        chosen = jnp.where(lane % 8 == tx, patterns[r, tx], chosen)
    one_hot = jnp.where((chosen == lane // 8) & (lane < 64), 1.0, 0.0).astype(F32)
    out[pl.ds(0, 256, stride=2), :] = modes + one_hot
    columns = pl.ds(pl.multiple_of(t // 2 * 128, 128), 128)
    first, last = w_ref[0:1, columns], w_ref[STRIP - 1 : STRIP, columns]
    first = jnp.where(t % 2 == 0, first, pltpu.roll(first, 64, axis=1))
    last = jnp.where(t % 2 == 0, pltpu.roll(last, 64, axis=1), last)
    edges = jnp.where(lane < 64, first, last)
    out[pl.ds(1, 256, stride=2), :] = jnp.broadcast_to(edges, (256, 128))


def face_fluxes(got, labels, intercept, sensitivity, own, first_ref, last_ref):
    lane = iota((16, 128), 1) < 64
    row = iota((16, 128), 0)
    totals = [jnp.zeros((16, 128), F32)] * 4
    for tx in range(8):
        columns = slice(tx * 128, tx * 128 + 128)
        left = got[tx * 32 : tx * 32 + 16]
        right = got[tx * 32 + 16 : tx * 32 + 32]
        first = jnp.where(lane, left, pltpu.roll(right, 64, axis=1))
        last = jnp.where(lane, pltpu.roll(left, 64, axis=1), right)
        first_ref[:, columns] = first
        last_ref[:, columns] = last
        base = jnp.zeros((16, 128), F32)
        slope = jnp.zeros((16, 128), F32)
        for ty in range(8):
            here = row // 2 == ty
            base = jnp.where(here, intercept[labels[ty, tx]], base)
            slope = jnp.where(here, sensitivity[labels[ty, tx]], slope)
        k_first = conductivity(first, base, slope)
        k_last = conductivity(last, base, slope)
        w_next = pltpu.roll(first, 15, axis=0)
        k_next = pltpu.roll(k_first, 15, axis=0)
        flux = jnp.where(row == 15, 0.0, 0.5 * (k_last + k_next) * (w_next - last))
        for q in range(4):
            totals[q] = totals[q] + own[q * 8 + tx : q * 8 + tx + 1, :] * flux
    sums = [jnp.sum(total, axis=1, keepdims=True) for total in totals]
    down = jnp.concatenate(sums, 0)
    up = jnp.concatenate([pltpu.roll(jnp.broadcast_to(x, (16, 128)), 1, axis=0) for x in sums], 0)
    return down, up[:, :1]


def cyclic_solve(force, rho, gain, store):
    even = iota(rho.shape, 0) < 4
    twice = 2.0 * rho
    square = rho * rho
    drives = [twice * force(tile) for tile in range(STEPS // 2)]
    pairs = [rho * pltpu.roll(drive, 4, axis=0) + drive for drive in drives]
    z = pairs[0]
    for pair in pairs[1:]:
        z = square * z + pair
    odd = gain * z
    for tile in range(STEPS // 2):
        before = rho * pltpu.roll(odd, 4, axis=0) + drives[tile]
        odd = square * odd + pairs[tile]
        store(tile, jnp.where(even, before, odd))


def make_factors(intercept, scales, device, factors):
    count = intercept.shape[0]
    conduct = intercept[0]
    for region in range(1, count):
        conduct = conduct + intercept[region]
    conduct = conduct / count
    lane = iota((1, SIZE), 1)
    row = iota((8, 128), 0) % 4
    mu = jnp.zeros((8, 128), F32)
    for q in range(4):
        chosen = jnp.where(lane == q * DEVICES + device, scales[0:1, :], 0.0)
        mu = jnp.where(row == q, jnp.sum(chosen, 1, keepdims=True), mu)
    weight = jnp.where((row == 0) & (device == 0), 1.0 / SIZE, 2.0 / SIZE)
    rho = 1.0 / (1.0 + 2.0 * (conduct * (scales[0:1, :] + CROSS_WEIGHT * mu[:, :1])))
    power = rho
    for _ in range(5):
        power = power * power
    factors[0:8, :] = rho
    factors[8:16, :] = ALPHA / (1.0 - ALPHA * power)
    factors[16:24, :] = scales[1:2, :] * weight[:, :1]


def weighted(tiles, scale):
    return stacked(jnp.concatenate([tile * scale for tile in tiles], 0))


def swap_rows(total, rows):
    for j in range(8):
        tiles = total[:, j * 128 : (j + 1) * 128].reshape(16, 8, 128)
        rows[:, j] = block_swap(tiles)


def first_solve_kernel(
    labels,
    intercept,
    sensitivity,
    received,
    tables,
    edge_table,
    scales,
    table_hi,
    table_lo,
    out,
    update,
    rest,
    near,
    factors,
    x_ref,
    rows,
    first_ref,
    last_ref,
):
    _, r, device = position()
    edges = received[pl.ds(1, 256, stride=2), :]
    group = pl.ds(pl.multiple_of(device // 16 * 16, 16), 16)
    mine = iota((16, SIZE), 0) == device % 16
    pieces = []
    for q in range(4):
        near_rows = table_hi[q, group, :].astype(F32) + table_lo[q, group, :].astype(F32)
        row = jnp.sum(jnp.where(mine, near_rows, 0.0), 0, keepdims=True)
        pieces += [row[:, tx * 128 : (tx + 1) * 128] for tx in range(8)]
    own = jnp.concatenate(pieces, 0)
    down, up = face_fluxes(edges, labels, intercept, sensitivity, own, first_ref, last_ref)
    strip = iota((16, SIZE), 0)
    near[0:1, :] = jnp.sum(jnp.where(strip == r - 1, last_ref[...], 0.0), 0, keepdims=True)
    near[1:2, :] = jnp.sum(jnp.where(strip == r + 1, first_ref[...], 0.0), 0, keepdims=True)
    near[2:8, :] = jnp.zeros((6, SIZE), F32)
    repeat = (iota((128, 32), 0) // 4 == iota((128, 32), 1)).astype(F32).astype(BF16)
    match = iota((128, 256), 0) % 4 == iota((128, 256), 1) // 64
    chosen = []
    for ty in range(8):
        part = received[pl.ds(2 * ty, 32, stride=16), :]
        part = jnp.where(iota((32, 128), 1) < 64, part, pltpu.roll(part, 64, axis=1)).astype(BF16)
        rows_nq = dot(repeat, jnp.concatenate([part, part], 1))
        chosen.append(jnp.where(match, rows_nq, 0.0).astype(BF16))
    chosen = jnp.concatenate(chosen, 0)
    by_tile = rows_by_table(stacked(own), *split(tables[...]), dot_nt)
    pieces = [
        by_tile[q * 8 : (q + 1) * 8, k * 128 : (k + 1) * 128] for q in range(4) for k in range(8)
    ]
    a_hi, a_lo = split(jnp.concatenate(pieces, 0))
    few = iota((64, 128), 1)
    inner = received[pl.ds(0, 64, stride=2), :]
    inner = inner + jnp.where(few == 127, down, 0.0) - jnp.where(few == 64, up, 0.0)
    top = jnp.where(few < 64, pltpu.roll(inner, 64, axis=1), 0.0)
    bottom = jnp.where(few < 64, 0.0, inner)
    d_hi, d_lo = split(jnp.concatenate([top, bottom], 0))
    to, source = iota((128, 128), 0), iota((128, 128), 1)
    same_mode = to % 4 == source // 16 % 4
    same_strip = source % 16 == 2 * (to // 16) + source // 64
    spread = (same_mode & same_strip).astype(F32).astype(BF16)
    power = dot(chosen, a_hi) + dot(chosen, a_lo)
    start = dot(spread, d_hi) + dot(spread, d_lo)
    for ty in range(8):
        parts = [power[ty * 128 : (ty + 1) * 128], start[ty * 16 : (ty + 1) * 16]]
        x_ref[:, ty * 128 : (ty + 1) * 128] = stacked(jnp.concatenate(parts, 0))

    make_factors(intercept, scales, device, factors)
    even = iota((8, P_BLOCK), 0) < 4
    total = jnp.zeros((128, SIZE), F32)
    edge_total = jnp.zeros((32, 128), F32)
    for block in range(4):
        lanes = slice(block * P_BLOCK, (block + 1) * P_BLOCK)
        high, low = table_hi[block], table_lo[block]
        modes = rows_by_table(x_ref[...], high, low, dot_nt)
        shared = modes[128:136]
        rho = factors[0:8, lanes]
        last = [jnp.zeros_like(rho)]
        tiles = []

        def force(tile):
            return modes[tile * 8 : tile * 8 + 8] + shared

        def store(tile, u):
            at = slice(tile * 8, tile * 8 + 8)
            update[at, lanes] = u
            turned = pltpu.roll(u, 4, axis=0)
            earlier = jnp.where(even, last[0], turned)
            rest[at, lanes] = modes[at] - 0.5 * (u - earlier)
            last[0] = turned
            tiles.append(u)

        cyclic_solve(force, rho, factors[8:16, lanes], store)
        u = weighted(tiles, factors[16:24, lanes])
        total = total + rows_by_table(u, high, low, dot)
        edge_total = edge_total + table_by_rows(edge_table[:32, lanes], edge_table[32:, lanes], u)

    swap_rows(total, rows)
    flat = rows.reshape(SIZE, 128)
    for q in range(4):
        out[pl.ds(q, 256, stride=5), :] = flat[pl.ds(q, 256, stride=4), :]
    low_lane = iota((16, 128), 1) < 8
    above, below = edge_total[0:16, :], edge_total[16:32, :]
    for t in range(16):
        left = pltpu.roll(above, (128 - 8 * t) % 128, axis=1)
        right = pltpu.roll(below, (136 - 8 * t) % 128, axis=1)
        out[pl.ds(80 * t + 4, 16, stride=5), :] = jnp.where(low_lane, left, right)


def second_solve_kernel(
    received, before, rest, factors, table_hi, table_lo, out, x_ref
):
    for j in range(8):
        tiles = block_swap(received[:, j])
        x_ref[:, j * 128 : (j + 1) * 128] = stacked(tiles.reshape(128, 128))
    total = jnp.zeros((128, SIZE), F32)
    for block in range(4):
        lanes = slice(block * P_BLOCK, (block + 1) * P_BLOCK)
        high, low = table_hi[block], table_lo[block]
        modes = rows_by_table(x_ref[...], high, low, dot_nt) + rest[:, lanes]
        rho = factors[0:8, lanes]
        tiles = []

        def force(tile):
            return modes[tile * 8 : tile * 8 + 8]

        def store(tile, u):
            tiles.append(u + before[tile * 8 : tile * 8 + 8, lanes])

        cyclic_solve(force, rho, factors[8:16, lanes], store)
        u = weighted(tiles, factors[16:24, lanes])
        total = total + rows_by_table(u, high, low, dot)
    swap_rows(total, out)


def final_kernel(received, table_hi, table_lo, initial, out):
    update = jnp.zeros((128, SIZE), F32)
    for q in range(4):
        rows = stacked(received[pl.ds(q, 256, stride=4), :].T)
        update = update + rows_by_table(rows, table_hi[q], table_lo[q], dot)
    start = initial[...]
    out[0] = update[:STRIP] + start
    out[1] = update[STRIP:] + start


def divergence_kernel(
    labels,
    intercept,
    sensitivity,
    received,
    initial,
    near,
    table_hi,
    table_lo,
    out,
    d_ref,
):
    _, r, _ = position()
    edge_rows = received[pl.ds(4, 256, stride=5), :].T[:16]
    owner = iota((16, 256), 0) % 4
    update = jnp.zeros((144, SIZE), F32)
    for q in range(4):
        inner = received[pl.ds(q, 256, stride=5), :].T
        masked = jnp.where(owner == q, edge_rows, 0.0)
        rows = stacked(jnp.concatenate([inner, masked], 0))
        update = update + rows_by_table(rows, table_hi[q], table_lo[q], dot)
    values = (intercept, sensitivity)
    first = r * STRIP
    own = material_rows(labels, values, first // TILE)
    above = material_rows(labels, values, jnp.maximum(first - 1, 0) // TILE)
    below = material_rows(labels, values, jnp.minimum(first + STRIP, SIZE - 1) // TILE)
    start = initial[...]
    for n in range(2):
        w = update[n * STRIP : (n + 1) * STRIP] + start
        k = conductivity(w, *own)
        at = 128 + 4 * n
        w_above = near[0:1, :] + jnp.sum(update[at : at + 4], 0, keepdims=True)
        w_below = near[1:2, :] + jnp.sum(update[at + 8 : at + 12], 0, keepdims=True)
        k_above = conductivity(w_above, *above)
        k_below = conductivity(w_below, *below)
        enter = 0.5 * (k_above + k[:1]) * (w[:1] - w_above)
        leave = 0.5 * (k_below + k[STRIP - 1 :]) * (w_below - w[STRIP - 1 :])
        enter = jnp.where(r == 0, 0.0, enter)
        leave = jnp.where(r == SIZE // STRIP - 1, 0.0, leave)
        d_ref[n * STRIP : (n + 1) * STRIP, :] = inner_divergence(w, k, enter, leave)
    d = stacked(d_ref[...])
    for q in range(4):
        out[pl.ds(q, 256, stride=4), :] = table_by_rows(table_hi[q], table_lo[q], d)


def whole(shape):
    return pl.BlockSpec(shape, lambda i: (0,) * len(shape))


SMEM = pl.BlockSpec(memory_space=pltpu.SMEM)


def call(kernel, limit, in_specs, outs, scratch, *args):
    results = pl.pallas_call(
        kernel,
        grid=(1,),
        in_specs=in_specs,
        out_specs=[whole(out) for out in outs],
        scratch_shapes=scratch,
        out_shape=[jax.ShapeDtypeStruct(out, F32) for out in outs],
        compiler_params=pltpu.CompilerParams(vmem_limit_bytes=limit),
    )(*args)
    return results if len(outs) > 1 else results[0]


def exchange(tiles, width):
    shape = (DEVICES, width // 128, 128) if width in (256, 512) else (DEVICES, 1, width)
    moved = lax.all_to_all(tiles.reshape(shape), BOTH, split_axis=0, concat_axis=0, tiled=True)
    return moved.reshape(-1, 128)


def shards(
    initial_warmth,
    pattern_choice,
    dissipation_tables,
    material_label,
    intercept_kappa,
    sensitivity_coef,
):
    made = constants()
    material = (material_label, intercept_kappa, sensitivity_coef)
    table = made["table"]
    one_number = pl.BlockSpec((None, 256, SIZE), lambda i: (lax.rem(lax.axis_index("tm"), 4), 0, 0))
    tables = [whole((4, 256, SIZE))] * 2
    strip = whole((STRIP, SIZE))
    field = whole((128, SIZE))
    few = whole((8, SIZE))
    sent = call(
        start_kernel,
        START_LIMIT,
        [SMEM] * 4 + [strip, one_number, one_number],
        [(512, 128)],
        [],
        *material,
        pattern_choice.reshape(16, 8),
        initial_warmth,
        *table,
    )
    received = exchange(sent, 256)
    sent, before, rest, near, factors = call(
        first_solve_kernel,
        VMEM_LIMIT,
        [SMEM] * 3
        + [
            whole((512, 128)),
            whole((SIZE, 128)),
            whole((64, SIZE)),
            few,
            *tables,
        ],
        [(1280, 128), (128, SIZE), (128, SIZE), (8, SIZE), (24, SIZE)],
        [
            pltpu.VMEM((288, SIZE), BF16),
            pltpu.VMEM((16, 8, 8, 128), F32),
            pltpu.VMEM((16, SIZE), F32),
            pltpu.VMEM((16, SIZE), F32),
        ],
        *material,
        received,
        dissipation_tables.reshape(SIZE, 128),
        made["edges"],
        made["scales"],
        *table,
    )
    received = exchange(sent, 640)
    sent = call(
        divergence_kernel,
        VMEM_LIMIT,
        [SMEM] * 3 + [whole((1280, 128)), strip, few, *tables],
        [(SIZE, 128)],
        [pltpu.VMEM((128, SIZE), F32)],
        *material,
        received,
        initial_warmth,
        near,
        *table,
    )
    received = exchange(sent, 512)
    sent = call(
        second_solve_kernel,
        VMEM_LIMIT,
        [whole((16, 8, 8, 128)), field, field, whole((24, SIZE)), *tables],
        [(16, 8, 8, 128)],
        [pltpu.VMEM((256, SIZE), BF16)],
        received.reshape(16, 8, 8, 128),
        before,
        rest,
        factors,
        *table,
    )
    received = exchange(sent, 512)
    return call(
        final_kernel,
        VMEM_LIMIT,
        [whole((SIZE, 128)), *tables, strip],
        [(2, STRIP, SIZE)],
        [],
        received,
        *table,
        initial_warmth,
    )


def solution(mesh):
    in_specs = (P("rows", None), P("tm", None, None), P(), P(), P(), P())
    out_specs = P("tm", "rows", None)
    return jax.shard_map(shards, mesh=mesh, in_specs=in_specs, out_specs=out_specs, check_vma=False)
```

```python
import functools
import math

import jax
import jax.numpy as jnp
import ml_dtypes
import numpy as np
from jax import lax
from jax.experimental import pallas as pl
from jax.experimental.pallas import tpu as pltpu
from jax.sharding import PartitionSpec as P

TILE = 128
SIZE = 1024
STEPS = 32
STRIP = 64
DEVICES = 256
ALPHA = 0.05
CROSS_WEIGHT = 1.0 / 64.0
P_BLOCK = 512
BOTH = ("tm", "rows")
F32 = jnp.float32
BF16 = jnp.bfloat16
VMEM_LIMIT = 24 * 1024 * 1024
START_LIMIT = 56 * 1024 * 1024


def halves(table):
    high = table.astype(ml_dtypes.bfloat16)
    low = (table - high.astype(np.float64)).astype(ml_dtypes.bfloat16)
    return high, low


@functools.cache
def constants():
    k = np.arange(SIZE, dtype=np.int64)
    phase = k[:, None] * (2 * k[None, :] + 1) % (4 * SIZE)
    cosines = np.cos(phase.astype(np.float64) * (math.pi / (2 * SIZE)))
    made = {}
    order = np.arange(SIZE).reshape(DEVICES, 4).T.reshape(-1)
    made["table"] = halves(cosines[order].reshape(4, DEVICES, SIZE))
    edge_rows = np.concatenate([np.arange(-1, SIZE - 1, STRIP), np.arange(STRIP, SIZE + 1, STRIP)])
    inside = (edge_rows >= 0) & (edge_rows < SIZE)
    edges = cosines.T[np.clip(edge_rows, 0, SIZE - 1)] * inside[:, None]
    made["edges"] = np.concatenate(halves(edges[:, order]), 0)
    scales = np.zeros((8, SIZE), np.float32)
    scales[0] = (2.0 - 2.0 * np.cos(np.arange(SIZE) * (math.pi / SIZE)))[order]
    scales[1] = 2.0 / SIZE
    scales[1, 0] = 1.0 / SIZE
    made["scales"] = scales
    return made


def split(values):
    high = values.astype(BF16)
    return high, (values - high.astype(F32)).astype(BF16)


def stacked(values):
    return jnp.concatenate(split(values), 0)


def dot(a, b):
    return jnp.dot(a, b, preferred_element_type=F32)


def dot_nt(a, b):
    return lax.dot_general(a, b, (((1,), (1,)), ((), ())), preferred_element_type=F32)


def rows_by_table(both, high, low, product):
    count = both.shape[0] // 2
    wide = product(both, high)
    return wide[:count] + wide[count:] + product(both[:count], low)


def table_by_rows(high, low, both):
    count = both.shape[0] // 2
    wide = dot_nt(high, both)
    return wide[:, :count] + wide[:, count:] + dot_nt(low, both[:count])


def iota(shape, dim):
    return lax.broadcasted_iota(jnp.int32, shape, dim)


def block_swap(tiles):
    shape = tiles.shape
    swapped = pltpu.roll(pltpu.roll(tiles, 4, axis=1), 64, axis=2)
    diagonal = (iota(shape, 1) < 4) == (iota(shape, 2) < 64)
    return jnp.where(diagonal, tiles, swapped)


def material_row(labels, values, ty):
    return jnp.concatenate(
        [jnp.full((1, TILE), values[labels[ty, tx]], F32) for tx in range(8)], 1
    )


def conductivity(values, base, slope):
    return base * (1.0 + slope * jnp.tanh(values))


def inner_divergence(w, k, above=None, below=None):
    shape = w.shape
    row, column = iota(shape, 0), iota(shape, 1)
    w_next = pltpu.roll(w, STRIP - 1, axis=0)
    k_next = pltpu.roll(k, STRIP - 1, axis=0)
    below = jnp.zeros((1, 1), F32) if below is None else below
    above = jnp.zeros((1, 1), F32) if above is None else above
    down = jnp.where(row == STRIP - 1, below, 0.5 * (k + k_next) * (w_next - w))
    up = jnp.where(row == 0, above, pltpu.roll(down, 1, axis=0))
    w_right = pltpu.roll(w, SIZE - 1, axis=1)
    k_right = pltpu.roll(k, SIZE - 1, axis=1)
    side = CROSS_WEIGHT * (0.5 * (k + k_right) * (w_right - w))
    side = jnp.where(column == SIZE - 1, 0.0, side)
    return down - up + (side - pltpu.roll(side, 1, axis=1))


def material_rows(labels, values, ty):
    return material_row(labels, values[0], ty), material_row(labels, values[1], ty)


def position():
    t, r = lax.axis_index("tm"), lax.axis_index("rows")
    return t, r, t * lax.axis_size("rows") + r


def start_kernel(
    labels,
    intercept,
    sensitivity,
    patterns,
    w_ref,
    table_hi,
    table_lo,
    out,
):
    t, r, _ = position()
    w = w_ref[...]
    base, slope = material_rows(labels, (intercept, sensitivity), r * STRIP // TILE)
    both = stacked(inner_divergence(w, conductivity(w, base, slope)))
    wide = dot_nt(table_hi[...], both)
    rest = dot_nt(table_lo[...], both)
    modes = wide + pltpu.roll(wide + rest, 64, axis=1)
    modes = jnp.where(iota((256, 128), 1) < 64, 0.0, modes)
    lane = iota((1, 128), 1)
    chosen = jnp.zeros((1, 128), jnp.int32)
    for tx in range(8):
        chosen = jnp.where(lane % 8 == tx, patterns[r, tx], chosen)
    one_hot = jnp.where((chosen == lane // 8) & (lane < 64), 1.0, 0.0).astype(F32)
    out[pl.ds(0, 256, stride=2), :] = modes + one_hot
    columns = pl.ds(pl.multiple_of(t // 2 * 128, 128), 128)
    first, last = w_ref[0:1, columns], w_ref[STRIP - 1 : STRIP, columns]
    first = jnp.where(t % 2 == 0, first, pltpu.roll(first, 64, axis=1))
    last = jnp.where(t % 2 == 0, pltpu.roll(last, 64, axis=1), last)
    edges = jnp.where(lane < 64, first, last)
    out[pl.ds(1, 256, stride=2), :] = jnp.broadcast_to(edges, (256, 128))


def face_fluxes(got, labels, intercept, sensitivity, own, first_ref, last_ref):
    lane = iota((16, 128), 1) < 64
    row = iota((16, 128), 0)
    totals = [jnp.zeros((16, 128), F32)] * 4
    for tx in range(8):
        columns = slice(tx * 128, tx * 128 + 128)
        left = got[tx * 32 : tx * 32 + 16]
        right = got[tx * 32 + 16 : tx * 32 + 32]
        first = jnp.where(lane, left, pltpu.roll(right, 64, axis=1))
        last = jnp.where(lane, pltpu.roll(left, 64, axis=1), right)
        first_ref[:, columns] = first
        last_ref[:, columns] = last
        base = jnp.zeros((16, 128), F32)
        slope = jnp.zeros((16, 128), F32)
        for ty in range(8):
            here = row // 2 == ty
            base = jnp.where(here, intercept[labels[ty, tx]], base)
            slope = jnp.where(here, sensitivity[labels[ty, tx]], slope)
        k_first = conductivity(first, base, slope)
        k_last = conductivity(last, base, slope)
        w_next = pltpu.roll(first, 15, axis=0)
        k_next = pltpu.roll(k_first, 15, axis=0)
        flux = jnp.where(row == 15, 0.0, 0.5 * (k_last + k_next) * (w_next - last))
        for q in range(4):
            totals[q] = totals[q] + own[q * 8 + tx : q * 8 + tx + 1, :] * flux
    sums = [jnp.sum(total, axis=1, keepdims=True) for total in totals]
    down = jnp.concatenate(sums, 0)
    up = jnp.concatenate([pltpu.roll(jnp.broadcast_to(x, (16, 128)), 1, axis=0) for x in sums], 0)
    return down, up[:, :1]


def cyclic_solve(force, rho, gain, store):
    even = iota(rho.shape, 0) < 4
    twice = 2.0 * rho
    square = rho * rho
    drives = [twice * force(tile) for tile in range(STEPS // 2)]
    pairs = [rho * pltpu.roll(drive, 4, axis=0) + drive for drive in drives]
    z = pairs[0]
    for pair in pairs[1:]:
        z = square * z + pair
    odd = gain * z
    for tile in range(STEPS // 2):
        before = rho * pltpu.roll(odd, 4, axis=0) + drives[tile]
        odd = square * odd + pairs[tile]
        store(tile, jnp.where(even, before, odd))


def make_factors(intercept, scales, device, factors):
    count = intercept.shape[0]
    conduct = intercept[0]
    for region in range(1, count):
        conduct = conduct + intercept[region]
    conduct = conduct / count
    lane = iota((1, SIZE), 1)
    row = iota((8, 128), 0) % 4
    mu = jnp.zeros((8, 128), F32)
    for q in range(4):
        chosen = jnp.where(lane == q * DEVICES + device, scales[0:1, :], 0.0)
        mu = jnp.where(row == q, jnp.sum(chosen, 1, keepdims=True), mu)
    weight = jnp.where((row == 0) & (device == 0), 1.0 / SIZE, 2.0 / SIZE)
    rho = 1.0 / (1.0 + 2.0 * (conduct * (scales[0:1, :] + CROSS_WEIGHT * mu[:, :1])))
    power = rho
    for _ in range(5):
        power = power * power
    factors[0:8, :] = rho
    factors[8:16, :] = ALPHA / (1.0 - ALPHA * power)
    factors[16:24, :] = scales[1:2, :] * weight[:, :1]


def weighted(tiles, scale):
    return stacked(jnp.concatenate([tile * scale for tile in tiles], 0))


def joined(table, first, count):
    numbers = slice(first // DEVICES, (first + count) // DEVICES)
    return table[numbers].reshape(count, SIZE)


def swap_rows(total, rows):
    for j in range(8):
        tiles = total[:, j * 128 : (j + 1) * 128].reshape(16, 8, 128)
        rows[:, j] = block_swap(tiles)


def first_solve_kernel(
    labels,
    intercept,
    sensitivity,
    received,
    tables,
    edge_table,
    scales,
    table_hi,
    table_lo,
    out,
    update,
    rest,
    near,
    factors,
    x_ref,
    rows,
    first_ref,
    last_ref,
):
    _, r, device = position()
    edges = received[pl.ds(1, 256, stride=2), :]
    group = pl.ds(pl.multiple_of(device // 16 * 16, 16), 16)
    mine = iota((16, SIZE), 0) == device % 16
    pieces = []
    for q in range(4):
        near_rows = table_hi[q, group, :].astype(F32) + table_lo[q, group, :].astype(F32)
        row = jnp.sum(jnp.where(mine, near_rows, 0.0), 0, keepdims=True)
        pieces += [row[:, tx * 128 : (tx + 1) * 128] for tx in range(8)]
    own = jnp.concatenate(pieces, 0)
    down, up = face_fluxes(edges, labels, intercept, sensitivity, own, first_ref, last_ref)
    strip = iota((16, SIZE), 0)
    near[0:1, :] = jnp.sum(jnp.where(strip == r - 1, last_ref[...], 0.0), 0, keepdims=True)
    near[1:2, :] = jnp.sum(jnp.where(strip == r + 1, first_ref[...], 0.0), 0, keepdims=True)
    near[2:8, :] = jnp.zeros((6, SIZE), F32)
    repeat = (iota((128, 32), 0) // 4 == iota((128, 32), 1)).astype(F32).astype(BF16)
    match = iota((128, 256), 0) % 4 == iota((128, 256), 1) // 64
    chosen = []
    for ty in range(8):
        part = received[pl.ds(2 * ty, 32, stride=16), :]
        part = jnp.where(iota((32, 128), 1) < 64, part, pltpu.roll(part, 64, axis=1)).astype(BF16)
        rows_nq = dot(repeat, jnp.concatenate([part, part], 1))
        chosen.append(jnp.where(match, rows_nq, 0.0).astype(BF16))
    chosen = jnp.concatenate(chosen, 0)
    by_tile = rows_by_table(stacked(own), *split(tables[...]), dot_nt)
    pieces = [
        by_tile[q * 8 : (q + 1) * 8, k * 128 : (k + 1) * 128] for q in range(4) for k in range(8)
    ]
    a_hi, a_lo = split(jnp.concatenate(pieces, 0))
    few = iota((64, 128), 1)
    inner = received[pl.ds(0, 64, stride=2), :]
    inner = inner + jnp.where(few == 127, down, 0.0) - jnp.where(few == 64, up, 0.0)
    top = jnp.where(few < 64, pltpu.roll(inner, 64, axis=1), 0.0)
    bottom = jnp.where(few < 64, 0.0, inner)
    d_hi, d_lo = split(jnp.concatenate([top, bottom], 0))
    to, source = iota((128, 128), 0), iota((128, 128), 1)
    same_mode = to % 4 == source // 16 % 4
    same_strip = source % 16 == 2 * (to // 16) + source // 64
    spread = (same_mode & same_strip).astype(F32).astype(BF16)
    power = dot(chosen, a_hi) + dot(chosen, a_lo)
    start = dot(spread, d_hi) + dot(spread, d_lo)
    for ty in range(8):
        parts = [power[ty * 128 : (ty + 1) * 128], start[ty * 16 : (ty + 1) * 16]]
        x_ref[:, ty * 128 : (ty + 1) * 128] = stacked(jnp.concatenate(parts, 0))

    make_factors(intercept, scales, device, factors)
    even = iota((8, P_BLOCK), 0) < 4
    total = jnp.zeros((128, SIZE), F32)
    edge_total = jnp.zeros((32, 128), F32)
    for block in range(SIZE // P_BLOCK):
        lanes = slice(block * P_BLOCK, (block + 1) * P_BLOCK)
        first = block * P_BLOCK
        high, low = joined(table_hi, first, P_BLOCK), joined(table_lo, first, P_BLOCK)
        modes = rows_by_table(x_ref[...], high, low, dot_nt)
        shared = modes[128:136]
        rho = factors[0:8, lanes]
        last = [jnp.zeros_like(rho)]
        tiles = []

        def force(tile):
            return modes[tile * 8 : tile * 8 + 8] + shared

        def store(tile, u):
            at = slice(tile * 8, tile * 8 + 8)
            update[at, lanes] = u
            turned = pltpu.roll(u, 4, axis=0)
            earlier = jnp.where(even, last[0], turned)
            rest[at, lanes] = modes[at] - 0.5 * (u - earlier)
            last[0] = turned
            tiles.append(u)

        cyclic_solve(force, rho, factors[8:16, lanes], store)
        u = weighted(tiles, factors[16:24, lanes])
        total = total + rows_by_table(u, high, low, dot)
        edge_total = edge_total + table_by_rows(edge_table[:32, lanes], edge_table[32:, lanes], u)

    swap_rows(total, rows)
    flat = rows.reshape(SIZE, 128)
    for q in range(4):
        out[pl.ds(q, 256, stride=5), :] = flat[pl.ds(q, 256, stride=4), :]
    low_lane = iota((16, 128), 1) < 8
    above, below = edge_total[0:16, :], edge_total[16:32, :]
    for t in range(16):
        left = pltpu.roll(above, (128 - 8 * t) % 128, axis=1)
        right = pltpu.roll(below, (136 - 8 * t) % 128, axis=1)
        out[pl.ds(80 * t + 4, 16, stride=5), :] = jnp.where(low_lane, left, right)


def second_solve_kernel(
    received, before, rest, factors, table_hi, table_lo, out, x_ref
):
    for j in range(8):
        tiles = block_swap(received[:, j])
        x_ref[:, j * 128 : (j + 1) * 128] = stacked(tiles.reshape(128, 128))
    total = jnp.zeros((128, SIZE), F32)
    for block in range(SIZE // P_BLOCK):
        lanes = slice(block * P_BLOCK, (block + 1) * P_BLOCK)
        first = block * P_BLOCK
        high, low = joined(table_hi, first, P_BLOCK), joined(table_lo, first, P_BLOCK)
        modes = rows_by_table(x_ref[...], high, low, dot_nt) + rest[:, lanes]
        rho = factors[0:8, lanes]
        tiles = []

        def force(tile):
            return modes[tile * 8 : tile * 8 + 8]

        def store(tile, u):
            tiles.append(u + before[tile * 8 : tile * 8 + 8, lanes])

        cyclic_solve(force, rho, factors[8:16, lanes], store)
        u = weighted(tiles, factors[16:24, lanes])
        total = total + rows_by_table(u, high, low, dot)
    swap_rows(total, out)


def final_kernel(received, table_hi, table_lo, initial, out):
    rows = [received[pl.ds(q, 256, stride=4), :].T for q in range(4)]
    high, low = joined(table_hi, 0, SIZE), joined(table_lo, 0, SIZE)
    update = rows_by_table(stacked(jnp.concatenate(rows, 1)), high, low, dot)
    start = initial[...]
    out[0] = update[:STRIP] + start
    out[1] = update[STRIP:] + start


def divergence_kernel(
    labels,
    intercept,
    sensitivity,
    received,
    initial,
    near,
    table_hi,
    table_lo,
    out,
    d_ref,
):
    _, r, _ = position()
    edge_rows = received[pl.ds(4, 256, stride=5), :].T[:16]
    owner = iota((16, 256), 0) % 4
    rows = []
    for q in range(4):
        inner = received[pl.ds(q, 256, stride=5), :].T
        masked = jnp.where(owner == q, edge_rows, 0.0)
        rows.append(jnp.concatenate([inner, masked], 0))
    high, low = joined(table_hi, 0, SIZE), joined(table_lo, 0, SIZE)
    update = rows_by_table(stacked(jnp.concatenate(rows, 1)), high, low, dot)
    values = (intercept, sensitivity)
    first = r * STRIP
    own = material_rows(labels, values, first // TILE)
    above = material_rows(labels, values, jnp.maximum(first - 1, 0) // TILE)
    below = material_rows(labels, values, jnp.minimum(first + STRIP, SIZE - 1) // TILE)
    start = initial[...]
    for n in range(2):
        w = update[n * STRIP : (n + 1) * STRIP] + start
        k = conductivity(w, *own)
        at = 128 + 4 * n
        w_above = near[0:1, :] + jnp.sum(update[at : at + 4], 0, keepdims=True)
        w_below = near[1:2, :] + jnp.sum(update[at + 8 : at + 12], 0, keepdims=True)
        k_above = conductivity(w_above, *above)
        k_below = conductivity(w_below, *below)
        enter = 0.5 * (k_above + k[:1]) * (w[:1] - w_above)
        leave = 0.5 * (k_below + k[STRIP - 1 :]) * (w_below - w[STRIP - 1 :])
        enter = jnp.where(r == 0, 0.0, enter)
        leave = jnp.where(r == SIZE // STRIP - 1, 0.0, leave)
        d_ref[n * STRIP : (n + 1) * STRIP, :] = inner_divergence(w, k, enter, leave)
    d = stacked(d_ref[...])
    for q in range(4):
        out[pl.ds(q, 256, stride=4), :] = table_by_rows(table_hi[q], table_lo[q], d)


def whole(shape):
    return pl.BlockSpec(shape, lambda i: (0,) * len(shape))


SMEM = pl.BlockSpec(memory_space=pltpu.SMEM)


def call(kernel, limit, in_specs, outs, scratch, *args):
    results = pl.pallas_call(
        kernel,
        grid=(1,),
        in_specs=in_specs,
        out_specs=[whole(out) for out in outs],
        scratch_shapes=scratch,
        out_shape=[jax.ShapeDtypeStruct(out, F32) for out in outs],
        compiler_params=pltpu.CompilerParams(vmem_limit_bytes=limit),
    )(*args)
    return results if len(outs) > 1 else results[0]


def exchange(tiles, width):
    shape = (DEVICES, width // 128, 128) if width in (256, 512) else (DEVICES, 1, width)
    moved = lax.all_to_all(tiles.reshape(shape), BOTH, split_axis=0, concat_axis=0, tiled=True)
    return moved.reshape(-1, 128)


def shards(
    initial_warmth,
    pattern_choice,
    dissipation_tables,
    material_label,
    intercept_kappa,
    sensitivity_coef,
):
    made = constants()
    material = (material_label, intercept_kappa, sensitivity_coef)
    table = made["table"]
    one_number = pl.BlockSpec((None, 256, SIZE), lambda i: (lax.rem(lax.axis_index("tm"), 4), 0, 0))
    tables = [whole((4, 256, SIZE))] * 2
    strip = whole((STRIP, SIZE))
    field = whole((128, SIZE))
    few = whole((8, SIZE))
    sent = call(
        start_kernel,
        START_LIMIT,
        [SMEM] * 4 + [strip, one_number, one_number],
        [(512, 128)],
        [],
        *material,
        pattern_choice.reshape(16, 8),
        initial_warmth,
        *table,
    )
    received = exchange(sent, 256)
    sent, before, rest, near, factors = call(
        first_solve_kernel,
        VMEM_LIMIT,
        [SMEM] * 3
        + [
            whole((512, 128)),
            whole((SIZE, 128)),
            whole((64, SIZE)),
            few,
            *tables,
        ],
        [(1280, 128), (128, SIZE), (128, SIZE), (8, SIZE), (24, SIZE)],
        [
            pltpu.VMEM((288, SIZE), BF16),
            pltpu.VMEM((16, 8, 8, 128), F32),
            pltpu.VMEM((16, SIZE), F32),
            pltpu.VMEM((16, SIZE), F32),
        ],
        *material,
        received,
        dissipation_tables.reshape(SIZE, 128),
        made["edges"],
        made["scales"],
        *table,
    )
    received = exchange(sent, 640)
    sent = call(
        divergence_kernel,
        VMEM_LIMIT,
        [SMEM] * 3 + [whole((1280, 128)), strip, few, *tables],
        [(SIZE, 128)],
        [pltpu.VMEM((128, SIZE), F32)],
        *material,
        received,
        initial_warmth,
        near,
        *table,
    )
    received = exchange(sent, 512)
    sent = call(
        second_solve_kernel,
        VMEM_LIMIT,
        [whole((16, 8, 8, 128)), field, field, whole((24, SIZE)), *tables],
        [(16, 8, 8, 128)],
        [pltpu.VMEM((256, SIZE), BF16)],
        received.reshape(16, 8, 8, 128),
        before,
        rest,
        factors,
        *table,
    )
    received = exchange(sent, 512)
    return call(
        final_kernel,
        VMEM_LIMIT,
        [whole((SIZE, 128)), *tables, strip],
        [(2, STRIP, SIZE)],
        [],
        received,
        *table,
        initial_warmth,
    )


def solution(mesh):
    in_specs = (P("rows", None), P("tm", None, None), P(), P(), P(), P())
    out_specs = P("tm", "rows", None)
    return jax.shard_map(shards, mesh=mesh, in_specs=in_specs, out_specs=out_specs, check_vma=False)
```

```python
import functools
import math

import jax
import jax.numpy as jnp
import ml_dtypes
import numpy as np
from jax import lax
from jax.experimental import pallas as pl
from jax.experimental.pallas import tpu as pltpu
from jax.sharding import PartitionSpec as P

TILE = 128
SIZE = 1024
STEPS = 32
STRIP = 64
DEVICES = 256
ALPHA = 0.05
CROSS_WEIGHT = 1.0 / 64.0
P_BLOCK = 1024
BOTH = ("tm", "rows")
F32 = jnp.float32
BF16 = jnp.bfloat16
VMEM_LIMIT = 24 * 1024 * 1024
START_LIMIT = 56 * 1024 * 1024


def halves(table):
    high = table.astype(ml_dtypes.bfloat16)
    low = (table - high.astype(np.float64)).astype(ml_dtypes.bfloat16)
    return high, low


@functools.cache
def constants():
    k = np.arange(SIZE, dtype=np.int64)
    phase = k[:, None] * (2 * k[None, :] + 1) % (4 * SIZE)
    cosines = np.cos(phase.astype(np.float64) * (math.pi / (2 * SIZE)))
    made = {}
    order = np.arange(SIZE).reshape(DEVICES, 4).T.reshape(-1)
    made["table"] = halves(cosines[order].reshape(4, DEVICES, SIZE))
    edge_rows = np.concatenate([np.arange(-1, SIZE - 1, STRIP), np.arange(STRIP, SIZE + 1, STRIP)])
    inside = (edge_rows >= 0) & (edge_rows < SIZE)
    edges = cosines.T[np.clip(edge_rows, 0, SIZE - 1)] * inside[:, None]
    made["edges"] = np.concatenate(halves(edges[:, order]), 0)
    scales = np.zeros((8, SIZE), np.float32)
    scales[0] = (2.0 - 2.0 * np.cos(np.arange(SIZE) * (math.pi / SIZE)))[order]
    scales[1] = 2.0 / SIZE
    scales[1, 0] = 1.0 / SIZE
    made["scales"] = scales
    return made


def split(values):
    high = values.astype(BF16)
    return high, (values - high.astype(F32)).astype(BF16)


def stacked(values):
    return jnp.concatenate(split(values), 0)


def dot(a, b):
    return jnp.dot(a, b, preferred_element_type=F32)


def dot_nt(a, b):
    return lax.dot_general(a, b, (((1,), (1,)), ((), ())), preferred_element_type=F32)


def rows_by_table(both, high, low, product):
    count = both.shape[0] // 2
    wide = product(both, high)
    return wide[:count] + wide[count:] + product(both[:count], low)


def table_by_rows(high, low, both):
    count = both.shape[0] // 2
    wide = dot_nt(high, both)
    return wide[:, :count] + wide[:, count:] + dot_nt(low, both[:count])


def iota(shape, dim):
    return lax.broadcasted_iota(jnp.int32, shape, dim)


def block_swap(tiles):
    shape = tiles.shape
    swapped = pltpu.roll(pltpu.roll(tiles, 4, axis=1), 64, axis=2)
    diagonal = (iota(shape, 1) < 4) == (iota(shape, 2) < 64)
    return jnp.where(diagonal, tiles, swapped)


def material_row(labels, values, ty):
    return jnp.concatenate(
        [jnp.full((1, TILE), values[labels[ty, tx]], F32) for tx in range(8)], 1
    )


def conductivity(values, base, slope):
    return base * (1.0 + slope * jnp.tanh(values))


def inner_divergence(w, k, above=None, below=None):
    shape = w.shape
    row, column = iota(shape, 0), iota(shape, 1)
    w_next = pltpu.roll(w, STRIP - 1, axis=0)
    k_next = pltpu.roll(k, STRIP - 1, axis=0)
    below = jnp.zeros((1, 1), F32) if below is None else below
    above = jnp.zeros((1, 1), F32) if above is None else above
    down = jnp.where(row == STRIP - 1, below, 0.5 * (k + k_next) * (w_next - w))
    up = jnp.where(row == 0, above, pltpu.roll(down, 1, axis=0))
    w_right = pltpu.roll(w, SIZE - 1, axis=1)
    k_right = pltpu.roll(k, SIZE - 1, axis=1)
    side = CROSS_WEIGHT * (0.5 * (k + k_right) * (w_right - w))
    side = jnp.where(column == SIZE - 1, 0.0, side)
    return down - up + (side - pltpu.roll(side, 1, axis=1))


def material_rows(labels, values, ty):
    return material_row(labels, values[0], ty), material_row(labels, values[1], ty)


def position():
    t, r = lax.axis_index("tm"), lax.axis_index("rows")
    return t, r, t * lax.axis_size("rows") + r


def start_kernel(
    labels,
    intercept,
    sensitivity,
    patterns,
    w_ref,
    table_hi,
    table_lo,
    out,
):
    t, r, _ = position()
    w = w_ref[...]
    base, slope = material_rows(labels, (intercept, sensitivity), r * STRIP // TILE)
    both = stacked(inner_divergence(w, conductivity(w, base, slope)))
    wide = dot_nt(table_hi[...], both)
    rest = dot_nt(table_lo[...], both)
    modes = wide + pltpu.roll(wide + rest, 64, axis=1)
    modes = jnp.where(iota((256, 128), 1) < 64, 0.0, modes)
    lane = iota((1, 128), 1)
    chosen = jnp.zeros((1, 128), jnp.int32)
    for tx in range(8):
        chosen = jnp.where(lane % 8 == tx, patterns[r, tx], chosen)
    one_hot = jnp.where((chosen == lane // 8) & (lane < 64), 1.0, 0.0).astype(F32)
    out[pl.ds(0, 256, stride=2), :] = modes + one_hot
    columns = pl.ds(pl.multiple_of(t // 2 * 128, 128), 128)
    first, last = w_ref[0:1, columns], w_ref[STRIP - 1 : STRIP, columns]
    first = jnp.where(t % 2 == 0, first, pltpu.roll(first, 64, axis=1))
    last = jnp.where(t % 2 == 0, pltpu.roll(last, 64, axis=1), last)
    edges = jnp.where(lane < 64, first, last)
    out[pl.ds(1, 256, stride=2), :] = jnp.broadcast_to(edges, (256, 128))


def face_fluxes(got, labels, intercept, sensitivity, own, first_ref, last_ref):
    lane = iota((16, 128), 1) < 64
    row = iota((16, 128), 0)
    totals = [jnp.zeros((16, 128), F32)] * 4
    for tx in range(8):
        columns = slice(tx * 128, tx * 128 + 128)
        left = got[tx * 32 : tx * 32 + 16]
        right = got[tx * 32 + 16 : tx * 32 + 32]
        first = jnp.where(lane, left, pltpu.roll(right, 64, axis=1))
        last = jnp.where(lane, pltpu.roll(left, 64, axis=1), right)
        first_ref[:, columns] = first
        last_ref[:, columns] = last
        base = jnp.zeros((16, 128), F32)
        slope = jnp.zeros((16, 128), F32)
        for ty in range(8):
            here = row // 2 == ty
            base = jnp.where(here, intercept[labels[ty, tx]], base)
            slope = jnp.where(here, sensitivity[labels[ty, tx]], slope)
        k_first = conductivity(first, base, slope)
        k_last = conductivity(last, base, slope)
        w_next = pltpu.roll(first, 15, axis=0)
        k_next = pltpu.roll(k_first, 15, axis=0)
        flux = jnp.where(row == 15, 0.0, 0.5 * (k_last + k_next) * (w_next - last))
        for q in range(4):
            totals[q] = totals[q] + own[q * 8 + tx : q * 8 + tx + 1, :] * flux
    sums = [jnp.sum(total, axis=1, keepdims=True) for total in totals]
    down = jnp.concatenate(sums, 0)
    up = jnp.concatenate([pltpu.roll(jnp.broadcast_to(x, (16, 128)), 1, axis=0) for x in sums], 0)
    return down, up[:, :1]


def cyclic_solve(force, rho, gain, store):
    even = iota(rho.shape, 0) < 4
    twice = 2.0 * rho
    square = rho * rho
    drives = [twice * force(tile) for tile in range(STEPS // 2)]
    pairs = [rho * pltpu.roll(drive, 4, axis=0) + drive for drive in drives]
    z = pairs[0]
    for pair in pairs[1:]:
        z = square * z + pair
    odd = gain * z
    for tile in range(STEPS // 2):
        before = rho * pltpu.roll(odd, 4, axis=0) + drives[tile]
        odd = square * odd + pairs[tile]
        store(tile, jnp.where(even, before, odd))


def make_factors(intercept, scales, device, factors):
    count = intercept.shape[0]
    conduct = intercept[0]
    for region in range(1, count):
        conduct = conduct + intercept[region]
    conduct = conduct / count
    lane = iota((1, SIZE), 1)
    row = iota((8, 128), 0) % 4
    mu = jnp.zeros((8, 128), F32)
    for q in range(4):
        chosen = jnp.where(lane == q * DEVICES + device, scales[0:1, :], 0.0)
        mu = jnp.where(row == q, jnp.sum(chosen, 1, keepdims=True), mu)
    weight = jnp.where((row == 0) & (device == 0), 1.0 / SIZE, 2.0 / SIZE)
    rho = 1.0 / (1.0 + 2.0 * (conduct * (scales[0:1, :] + CROSS_WEIGHT * mu[:, :1])))
    power = rho
    for _ in range(5):
        power = power * power
    factors[0:8, :] = rho
    factors[8:16, :] = ALPHA / (1.0 - ALPHA * power)
    factors[16:24, :] = scales[1:2, :] * weight[:, :1]


def weighted(tiles, scale):
    return stacked(jnp.concatenate([tile * scale for tile in tiles], 0))


def joined(table, first, count):
    numbers = slice(first // DEVICES, (first + count) // DEVICES)
    return table[numbers].reshape(count, SIZE)


def swap_rows(total, rows):
    for j in range(8):
        tiles = total[:, j * 128 : (j + 1) * 128].reshape(16, 8, 128)
        rows[:, j] = block_swap(tiles)


def first_solve_kernel(
    labels,
    intercept,
    sensitivity,
    received,
    tables,
    edge_table,
    scales,
    table_hi,
    table_lo,
    out,
    update,
    rest,
    near,
    factors,
    x_ref,
    rows,
    first_ref,
    last_ref,
):
    _, r, device = position()
    edges = received[pl.ds(1, 256, stride=2), :]
    group = pl.ds(pl.multiple_of(device // 16 * 16, 16), 16)
    mine = iota((16, SIZE), 0) == device % 16
    pieces = []
    for q in range(4):
        near_rows = table_hi[q, group, :].astype(F32) + table_lo[q, group, :].astype(F32)
        row = jnp.sum(jnp.where(mine, near_rows, 0.0), 0, keepdims=True)
        pieces += [row[:, tx * 128 : (tx + 1) * 128] for tx in range(8)]
    own = jnp.concatenate(pieces, 0)
    down, up = face_fluxes(edges, labels, intercept, sensitivity, own, first_ref, last_ref)
    strip = iota((16, SIZE), 0)
    near[0:1, :] = jnp.sum(jnp.where(strip == r - 1, last_ref[...], 0.0), 0, keepdims=True)
    near[1:2, :] = jnp.sum(jnp.where(strip == r + 1, first_ref[...], 0.0), 0, keepdims=True)
    near[2:8, :] = jnp.zeros((6, SIZE), F32)
    repeat = (iota((128, 32), 0) // 4 == iota((128, 32), 1)).astype(F32).astype(BF16)
    match = iota((128, 256), 0) % 4 == iota((128, 256), 1) // 64
    chosen = []
    for ty in range(8):
        part = received[pl.ds(2 * ty, 32, stride=16), :]
        part = jnp.where(iota((32, 128), 1) < 64, part, pltpu.roll(part, 64, axis=1)).astype(BF16)
        rows_nq = dot(repeat, jnp.concatenate([part, part], 1))
        chosen.append(jnp.where(match, rows_nq, 0.0).astype(BF16))
    chosen = jnp.concatenate(chosen, 0)
    by_tile = rows_by_table(stacked(own), *split(tables[...]), dot_nt)
    pieces = [
        by_tile[q * 8 : (q + 1) * 8, k * 128 : (k + 1) * 128] for q in range(4) for k in range(8)
    ]
    a_hi, a_lo = split(jnp.concatenate(pieces, 0))
    few = iota((64, 128), 1)
    inner = received[pl.ds(0, 64, stride=2), :]
    inner = inner + jnp.where(few == 127, down, 0.0) - jnp.where(few == 64, up, 0.0)
    top = jnp.where(few < 64, pltpu.roll(inner, 64, axis=1), 0.0)
    bottom = jnp.where(few < 64, 0.0, inner)
    d_hi, d_lo = split(jnp.concatenate([top, bottom], 0))
    to, source = iota((128, 128), 0), iota((128, 128), 1)
    same_mode = to % 4 == source // 16 % 4
    same_strip = source % 16 == 2 * (to // 16) + source // 64
    spread = (same_mode & same_strip).astype(F32).astype(BF16)
    power = dot(chosen, a_hi) + dot(chosen, a_lo)
    start = dot(spread, d_hi) + dot(spread, d_lo)
    for ty in range(8):
        parts = [power[ty * 128 : (ty + 1) * 128], start[ty * 16 : (ty + 1) * 16]]
        x_ref[:, ty * 128 : (ty + 1) * 128] = stacked(jnp.concatenate(parts, 0))

    make_factors(intercept, scales, device, factors)
    even = iota((8, P_BLOCK), 0) < 4
    total = jnp.zeros((128, SIZE), F32)
    edge_total = jnp.zeros((32, 128), F32)
    for block in range(SIZE // P_BLOCK):
        lanes = slice(block * P_BLOCK, (block + 1) * P_BLOCK)
        first = block * P_BLOCK
        high, low = joined(table_hi, first, P_BLOCK), joined(table_lo, first, P_BLOCK)
        modes = rows_by_table(x_ref[...], high, low, dot_nt)
        shared = modes[128:136]
        rho = factors[0:8, lanes]
        last = [jnp.zeros_like(rho)]
        tiles = []

        def force(tile):
            return modes[tile * 8 : tile * 8 + 8] + shared

        def store(tile, u):
            at = slice(tile * 8, tile * 8 + 8)
            update[at, lanes] = u
            turned = pltpu.roll(u, 4, axis=0)
            earlier = jnp.where(even, last[0], turned)
            rest[at, lanes] = modes[at] - 0.5 * (u - earlier)
            last[0] = turned
            tiles.append(u)

        cyclic_solve(force, rho, factors[8:16, lanes], store)
        u = weighted(tiles, factors[16:24, lanes])
        total = total + rows_by_table(u, high, low, dot)
        edge_total = edge_total + table_by_rows(edge_table[:32, lanes], edge_table[32:, lanes], u)

    swap_rows(total, rows)
    flat = rows.reshape(SIZE, 128)
    for q in range(4):
        out[pl.ds(q, 256, stride=5), :] = flat[pl.ds(q, 256, stride=4), :]
    low_lane = iota((16, 128), 1) < 8
    above, below = edge_total[0:16, :], edge_total[16:32, :]
    for t in range(16):
        left = pltpu.roll(above, (128 - 8 * t) % 128, axis=1)
        right = pltpu.roll(below, (136 - 8 * t) % 128, axis=1)
        out[pl.ds(80 * t + 4, 16, stride=5), :] = jnp.where(low_lane, left, right)


def second_solve_kernel(
    received, before, rest, factors, table_hi, table_lo, out, x_ref
):
    for j in range(8):
        tiles = block_swap(received[:, j])
        x_ref[:, j * 128 : (j + 1) * 128] = stacked(tiles.reshape(128, 128))
    total = jnp.zeros((128, SIZE), F32)
    for block in range(SIZE // P_BLOCK):
        lanes = slice(block * P_BLOCK, (block + 1) * P_BLOCK)
        first = block * P_BLOCK
        high, low = joined(table_hi, first, P_BLOCK), joined(table_lo, first, P_BLOCK)
        modes = rows_by_table(x_ref[...], high, low, dot_nt) + rest[:, lanes]
        rho = factors[0:8, lanes]
        tiles = []

        def force(tile):
            return modes[tile * 8 : tile * 8 + 8]

        def store(tile, u):
            tiles.append(u + before[tile * 8 : tile * 8 + 8, lanes])

        cyclic_solve(force, rho, factors[8:16, lanes], store)
        u = weighted(tiles, factors[16:24, lanes])
        total = total + rows_by_table(u, high, low, dot)
    swap_rows(total, out)


def final_kernel(received, table_hi, table_lo, initial, out):
    rows = [received[pl.ds(q, 256, stride=4), :].T for q in range(4)]
    high, low = joined(table_hi, 0, SIZE), joined(table_lo, 0, SIZE)
    update = rows_by_table(stacked(jnp.concatenate(rows, 1)), high, low, dot)
    start = initial[...]
    out[0] = update[:STRIP] + start
    out[1] = update[STRIP:] + start


def divergence_kernel(
    labels,
    intercept,
    sensitivity,
    received,
    initial,
    near,
    table_hi,
    table_lo,
    out,
    d_ref,
):
    _, r, _ = position()
    edge_rows = received[pl.ds(4, 256, stride=5), :].T[:16]
    owner = iota((16, 256), 0) % 4
    rows = []
    for q in range(4):
        inner = received[pl.ds(q, 256, stride=5), :].T
        masked = jnp.where(owner == q, edge_rows, 0.0)
        rows.append(jnp.concatenate([inner, masked], 0))
    high, low = joined(table_hi, 0, SIZE), joined(table_lo, 0, SIZE)
    update = rows_by_table(stacked(jnp.concatenate(rows, 1)), high, low, dot)
    values = (intercept, sensitivity)
    first = r * STRIP
    own = material_rows(labels, values, first // TILE)
    above = material_rows(labels, values, jnp.maximum(first - 1, 0) // TILE)
    below = material_rows(labels, values, jnp.minimum(first + STRIP, SIZE - 1) // TILE)
    start = initial[...]
    for n in range(2):
        w = update[n * STRIP : (n + 1) * STRIP] + start
        k = conductivity(w, *own)
        at = 128 + 4 * n
        w_above = near[0:1, :] + jnp.sum(update[at : at + 4], 0, keepdims=True)
        w_below = near[1:2, :] + jnp.sum(update[at + 8 : at + 12], 0, keepdims=True)
        k_above = conductivity(w_above, *above)
        k_below = conductivity(w_below, *below)
        enter = 0.5 * (k_above + k[:1]) * (w[:1] - w_above)
        leave = 0.5 * (k_below + k[STRIP - 1 :]) * (w_below - w[STRIP - 1 :])
        enter = jnp.where(r == 0, 0.0, enter)
        leave = jnp.where(r == SIZE // STRIP - 1, 0.0, leave)
        d_ref[n * STRIP : (n + 1) * STRIP, :] = inner_divergence(w, k, enter, leave)
    d = stacked(d_ref[...])
    for q in range(4):
        out[pl.ds(q, 256, stride=4), :] = table_by_rows(table_hi[q], table_lo[q], d)


def whole(shape):
    return pl.BlockSpec(shape, lambda i: (0,) * len(shape))


SMEM = pl.BlockSpec(memory_space=pltpu.SMEM)


def call(kernel, limit, in_specs, outs, scratch, *args):
    results = pl.pallas_call(
        kernel,
        grid=(1,),
        in_specs=in_specs,
        out_specs=[whole(out) for out in outs],
        scratch_shapes=scratch,
        out_shape=[jax.ShapeDtypeStruct(out, F32) for out in outs],
        compiler_params=pltpu.CompilerParams(vmem_limit_bytes=limit),
    )(*args)
    return results if len(outs) > 1 else results[0]


def exchange(tiles, width):
    shape = (DEVICES, width // 128, 128) if width in (256, 512) else (DEVICES, 1, width)
    moved = lax.all_to_all(tiles.reshape(shape), BOTH, split_axis=0, concat_axis=0, tiled=True)
    return moved.reshape(-1, 128)


def shards(
    initial_warmth,
    pattern_choice,
    dissipation_tables,
    material_label,
    intercept_kappa,
    sensitivity_coef,
):
    made = constants()
    material = (material_label, intercept_kappa, sensitivity_coef)
    table = made["table"]
    one_number = pl.BlockSpec((None, 256, SIZE), lambda i: (lax.rem(lax.axis_index("tm"), 4), 0, 0))
    tables = [whole((4, 256, SIZE))] * 2
    strip = whole((STRIP, SIZE))
    field = whole((128, SIZE))
    few = whole((8, SIZE))
    sent = call(
        start_kernel,
        START_LIMIT,
        [SMEM] * 4 + [strip, one_number, one_number],
        [(512, 128)],
        [],
        *material,
        pattern_choice.reshape(16, 8),
        initial_warmth,
        *table,
    )
    received = exchange(sent, 256)
    sent, before, rest, near, factors = call(
        first_solve_kernel,
        VMEM_LIMIT,
        [SMEM] * 3
        + [
            whole((512, 128)),
            whole((SIZE, 128)),
            whole((64, SIZE)),
            few,
            *tables,
        ],
        [(1280, 128), (128, SIZE), (128, SIZE), (8, SIZE), (24, SIZE)],
        [
            pltpu.VMEM((288, SIZE), BF16),
            pltpu.VMEM((16, 8, 8, 128), F32),
            pltpu.VMEM((16, SIZE), F32),
            pltpu.VMEM((16, SIZE), F32),
        ],
        *material,
        received,
        dissipation_tables.reshape(SIZE, 128),
        made["edges"],
        made["scales"],
        *table,
    )
    received = exchange(sent, 640)
    sent = call(
        divergence_kernel,
        VMEM_LIMIT,
        [SMEM] * 3 + [whole((1280, 128)), strip, few, *tables],
        [(SIZE, 128)],
        [pltpu.VMEM((128, SIZE), F32)],
        *material,
        received,
        initial_warmth,
        near,
        *table,
    )
    received = exchange(sent, 512)
    sent = call(
        second_solve_kernel,
        VMEM_LIMIT,
        [whole((16, 8, 8, 128)), field, field, whole((24, SIZE)), *tables],
        [(16, 8, 8, 128)],
        [pltpu.VMEM((256, SIZE), BF16)],
        received.reshape(16, 8, 8, 128),
        before,
        rest,
        factors,
        *table,
    )
    received = exchange(sent, 512)
    return call(
        final_kernel,
        VMEM_LIMIT,
        [whole((SIZE, 128)), *tables, strip],
        [(2, STRIP, SIZE)],
        [],
        received,
        *table,
        initial_warmth,
    )


def solution(mesh):
    in_specs = (P("rows", None), P("tm", None, None), P(), P(), P(), P())
    out_specs = P("tm", "rows", None)
    return jax.shard_map(shards, mesh=mesh, in_specs=in_specs, out_specs=out_specs, check_vma=False)
```
